128 devices in a mesh: gx: 8 (over z, core), gy: 16 (over x, y).
Axes of the slice: x: 4, y: 4, z: 4, core: 2. Of those that a mesh axis runs over, the one named last changes fastest.
Arguments:
- solvent_pos: float32 [3, 1572864], P(None, ('gx', 'gy')), may hold values from 0 to 48, as said below
- solvent_vel: float32 [3, 1572864], P(None, ('gx', 'gy')), may hold values from -6 to 6
- pair_index: int32 [49152, 128], P(('gx', 'gy')), may hold values from 0 to 110592, as said below
- random_pairs: bfloat16 [49152, 128, 128], P(('gx', 'gy')), may hold values from -4 to 4
- membrane_pos: float32 [3, 1314816], P(None, ('gx', 'gy')), may hold values from 0 to 48, as said below
- membrane_vel: float32 [3, 1314816], P(None, ('gx', 'gy')), may hold values from -6 to 6
- mem_vertex: int32 [8192, 128], P(('gx', 'gy')), may hold values from 0 to 10271, as said below
- mem_partner: int32 [8192, 128], P(('gx', 'gy')), may hold values from 0 to 110591, as said below
- bending: float32 [642, 642], replicated, may hold values from -1 to 2
- rest_size: float32 [2048], P(('gx', 'gy')), may hold values from 2 to 8
- cell_count: int32 [128], P(('gx', 'gy')), may hold values from 1 to 16, as said below
Outputs:
- solvent_velocity: float32 [3, 1572864], P(None, ('gx', 'gy'))
- membrane_velocity: float32 [3, 1314816], P(None, ('gx', 'gy'))
The draws below stay inside these ranges and needn't reach their ends.
Inputs may be any that keep to these rules, and one draw needn't show every extreme that they name: `solvent_pos`: positions lie in the owning brick's frame: x and y in [0, 4), z in [0, 48); particle m lies in box b = m // 128, the cube of side 2 with corner (2 (b % 2), 2 (b // 2 % 2), 2 (b // 4)). `membrane_pos`: vertex positions lie in the owning brick's frame: x and y in [0, 4), z in [0, 48). `pair_index`: index (3 p + q) * 12288 + m names particle m of brick (i + p - 1, j + q - 1); 110592 marks an empty slot. `mem_vertex`: index c * 642 + v names vertex v of the brick's cell slot c. `mem_partner`: index (3 p + q) * 12288 + m names particle m of brick (i + p - 1, j + q - 1). Cell slots 0 to cell_count - 1 of a brick are live.
All inputs are finite; a program needn't handle non-finite values.
Results may differ from the reference program's by a relative error of at most 0.0003.
Values sent between devices are 32-bit elements; how exact they have to be, the bound alone decides.
A program may use at most 448 MiB of HBM per device.

```python
import math
import jax
import jax.numpy as jnp
from jax import lax

V = 642
TILE = 128
PAIRS = 4
BOXES = 96
CELL_DEV = 16
MEM_TILES = 64
P_DEV = 12288
BRICKS = 128
NP = 1572864
TILES_DEV = 384
ALL_TILES = 49152
CELLS = 2048
N_GX = 8
N_GY = 16


def box_corner(box_index):
    along_x = (box_index % 2).astype(jnp.float32) * 2.0
    along_y = (box_index // 2 % 2).astype(jnp.float32) * 2.0
    along_z = (box_index // 4).astype(jnp.float32) * 2.0
    return jnp.stack([along_x, along_y, along_z], axis=0)


def cell_boxes(key):
    return jax.random.randint(jax.random.fold_in(key, 901), (BRICKS, CELL_DEV), 0, BOXES)


def tile_cells(key):
    return jax.random.randint(jax.random.fold_in(key, 907), (BRICKS, MEM_TILES), 0, CELL_DEV)


def nearby_box(key, box_index):
    steps = jax.random.randint(key, (3,) + box_index.shape, -1, 2)
    still = (steps[0] == 0) & (steps[1] == 0) & (steps[2] == 0)
    step_x = jnp.where(still, 1, steps[0])
    reach_x = box_index % 2 + step_x
    reach_y = box_index // 2 % 2 + steps[1]
    reach_z = jnp.clip(box_index // 4 + steps[2], 0, BOXES // 4 - 1)
    direction = (1 + reach_x // 2) * 3 + (1 + reach_y // 2)
    target = reach_z * 4 + reach_y % 2 * 2 + reach_x % 2
    return (direction, target)


def draw_solvent_pos(key, part):
    key = jax.random.fold_in(key, 11)
    corner = box_corner(jnp.arange(P_DEV, dtype=jnp.int32) // TILE)
    jitter = jax.random.uniform(key, (3, BRICKS, P_DEV), jnp.float32, 0.0, 2.0)
    return (corner[:, None, :] + jitter).reshape(3, NP)


def draw_pair_index(key, part):
    key = jax.random.fold_in(key, 23)
    first_key, second_key, third_key = jax.random.split(key, 3)
    tile_ids = jnp.arange(TILES_DEV, dtype=jnp.int32)
    box_ids = jnp.broadcast_to((tile_ids // PAIRS)[None, :], (BRICKS, TILES_DEV))
    direction, target = nearby_box(first_key, box_ids)
    own_box = (tile_ids % 2 == 1)[None, :]
    direction = jnp.where(own_box, 4, direction)
    target = jnp.where(own_box, box_ids, target)
    members = jax.random.randint(second_key, (BRICKS, TILES_DEV, TILE), 0, TILE)
    listed = (direction * P_DEV + target * TILE)[:, :, None] + members
    filled = jax.random.randint(third_key, (BRICKS, TILES_DEV, 1), TILE * 3 // 4, TILE + 1)
    filled = filled.at[:, 0].set(TILE * 3 // 4)
    slots = jnp.arange(TILE, dtype=jnp.int32)[None, None, :]
    listed = jnp.where(slots < filled, listed, 9 * P_DEV)
    return listed.reshape(BRICKS * TILES_DEV, TILE).astype(jnp.int32)


def draw_membrane_pos(key, part):
    boxes = cell_boxes(key)
    key = jax.random.fold_in(key, 37)
    corner = box_corner(boxes)
    jitter = jax.random.uniform(key, (3, BRICKS, CELL_DEV, V), jnp.float32, 0.0, 2.0)
    return (corner[:, :, :, None] + jitter).reshape(3, CELLS * V)


def draw_mem_vertex(key, part):
    cells = tile_cells(key)
    key = jax.random.fold_in(key, 41)
    vertices = jax.random.randint(key, (BRICKS, MEM_TILES, TILE), 0, V)
    return (cells[:, :, None] * V + vertices).reshape(BRICKS * MEM_TILES, TILE).astype(jnp.int32)


def draw_mem_partner(key, part):
    boxes = cell_boxes(key)
    cells = tile_cells(key)
    key = jax.random.fold_in(key, 53)
    first_key, second_key = jax.random.split(key, 2)
    home = jnp.take_along_axis(boxes, cells, axis=1)
    direction, target = nearby_box(first_key, home)
    own_box = (jnp.arange(MEM_TILES, dtype=jnp.int32) % 2 == 0)[None, :]
    direction = jnp.where(own_box, 4, direction)
    target = jnp.where(own_box, home, target)
    members = jax.random.randint(second_key, (BRICKS, MEM_TILES, TILE), 0, TILE)
    listed = (direction * P_DEV + target * TILE)[:, :, None] + members
    return listed.reshape(BRICKS * MEM_TILES, TILE).astype(jnp.int32)


def draw_bending(key, part):
    key = jax.random.fold_in(key, 71)
    first_key, second_key = jax.random.split(key, 2)
    spread_part = jax.random.uniform(first_key, (V, V), jnp.float32, -1.0, 1.0) * (1.0 / math.sqrt(V))
    diagonal = jax.random.uniform(second_key, (V,), jnp.float32, 1.0, 2.0)
    on_diagonal = jnp.arange(V)[:, None] == jnp.arange(V)[None, :]
    return jnp.where(on_diagonal, diagonal[:, None], spread_part)


def draw_cell_count(key, part):
    key = jax.random.fold_in(key, 61)
    first_key, second_key, third_key = jax.random.split(key, 3)
    base = jax.random.randint(first_key, (BRICKS,), 1, CELL_DEV // 2 + 1)
    crowded = jax.random.randint(second_key, (BRICKS,), 0, 4) == 0
    counts = jnp.where(crowded, CELL_DEV, base)
    counts = counts.at[jax.random.randint(third_key, (), 0, BRICKS)].set(CELL_DEV)
    return counts.astype(jnp.int32)


def block_scale(stream_key, shape, shards, least, largest):
    factor_of, own = 1.0, jax.random.fold_in(stream_key, 6)
    for position, blocks in shards:
        heights = jnp.exp(jax.random.uniform(jax.random.fold_in(own, position), (blocks,), jnp.float32, least / len(shards), largest / len(shards)))
        factor_of = factor_of * jnp.repeat(heights, shape[position] // blocks).reshape([-1 if axis == position else 1 for axis in range(len(shape))])
    return factor_of


def centred(own_key, extent, scale, most, shards=(), kind=jnp.bfloat16):
    drawn = jax.random.normal(own_key, extent, jnp.float32) * scale
    if len(shards) > 0:
        drawn = block_scale(own_key, extent, shards, -0.22, 0.18) * drawn
    return jnp.clip(drawn, min=-most, max=most).astype(kind)


def setup_inputs(seed: int = 0) -> dict:
    arg_keys = jax.random.split(jax.random.key(seed), 12)
    return {
        "solvent_pos": draw_solvent_pos(jax.random.fold_in(arg_keys[11], 71), 0),
        "solvent_vel": centred(arg_keys[1], (3, NP), 1.0, 6.0, ((1, 128),), jnp.float32),
        "pair_index": draw_pair_index(jax.random.fold_in(arg_keys[11], 71), 0),
        "random_pairs": centred(arg_keys[3], (ALL_TILES, TILE, TILE), 1.0, 4.0, ((0, 128),)),
        "membrane_pos": draw_membrane_pos(jax.random.fold_in(arg_keys[11], 71), 0),
        "membrane_vel": centred(arg_keys[5], (3, CELLS * V), 1.0, 6.0, ((1, 128),), jnp.float32),
        "mem_vertex": draw_mem_vertex(jax.random.fold_in(arg_keys[11], 71), 0),
        "mem_partner": draw_mem_partner(jax.random.fold_in(arg_keys[11], 71), 0),
        "bending": draw_bending(jax.random.fold_in(arg_keys[11], 71), 0),
        "rest_size": jnp.clip(jnp.exp(math.log(8.0) - 1.3862944 * jax.random.uniform(arg_keys[9], (CELLS,), jnp.float32) ** block_scale(arg_keys[9], (CELLS,), ((0, 128),), -0.2, 0.2)), 2.0, 8.0),
        "cell_count": draw_cell_count(jax.random.fold_in(arg_keys[11], 71), 0),
    }


TIME_STEP = 0.01
REPEL_STRENGTH = 25.0
FRICTION = 4.5
NOISE_SCALE = 30.0
BENDING_MODULUS = 20.0
AREA_MODULUS = 40.0
SOLVENT_PUSH = 0.5
RADIUS_FLOOR = 0.1
BRICK_SIDE = 4.0
FAR_AWAY = 1000.0

def pair_terms(left_pos, left_vel, right_pos, right_vel, noise_block):
    offset = left_pos[..., :, None] - right_pos[..., None, :]
    radius = jnp.sqrt(lax.optimization_barrier(jnp.sum(offset * offset, axis=0)))
    weight = jnp.maximum(1.0 - radius, 0.0)
    direction_unit = offset / jnp.maximum(radius, RADIUS_FLOOR)
    approach = lax.optimization_barrier(jnp.sum(direction_unit * (left_vel[..., :, None] - right_vel[..., None, :]), axis=0))
    magnitude = weight * (REPEL_STRENGTH - FRICTION * weight * approach + NOISE_SCALE * noise_block)
    return magnitude[None] * direction_unit

def neighbourhood(extended):
    shifts = (jnp.arange(3, dtype=jnp.int32) - 1).astype(jnp.float32) * BRICK_SIDE
    offsets = jnp.stack([jnp.broadcast_to(shifts[:, None], (3, 3)), jnp.broadcast_to(shifts[None, :], (3, 3)), jnp.zeros((3, 3), jnp.float32)], axis=2)
    positions = extended[:, :, 0:3] + offsets[:, :, :, None]
    velocity = extended[:, :, 3:6]
    span = 9 * extended.shape[3]
    flat_pos = positions.transpose(2, 0, 1, 3).reshape(3, span)
    flat_vel = velocity.transpose(2, 0, 1, 3).reshape(3, span)
    flat_pos = jnp.concatenate([flat_pos, jnp.full((3, 1), FAR_AWAY, jnp.float32)], axis=1)
    flat_vel = jnp.concatenate([flat_vel, jnp.zeros((3, 1), jnp.float32)], axis=1)
    return (flat_pos, flat_vel)

def solvent_forces(own_pos, own_vel, flat_pos, flat_vel, pair_index, random_pairs):
    tiles_here = pair_index.shape[0]
    group_size = math.gcd(tiles_here, 16)
    box_count = group_size // PAIRS

    def add_group(loop_turn, force):
        tile_start = (loop_turn * group_size).astype(jnp.int32)
        chosen = lax.dynamic_slice_in_dim(pair_index, tile_start, group_size, 0)
        noise_block = lax.dynamic_slice_in_dim(random_pairs, tile_start, group_size, 0).astype(jnp.float32)
        row_start = tile_start // PAIRS * TILE
        left_pos = lax.dynamic_slice_in_dim(own_pos, row_start, box_count * TILE, 1).reshape(3, box_count, 1, TILE)
        left_pos = jnp.broadcast_to(left_pos, (3, box_count, PAIRS, TILE)).reshape(3, group_size, TILE)
        left_vel = lax.dynamic_slice_in_dim(own_vel, row_start, box_count * TILE, 1).reshape(3, box_count, 1, TILE)
        left_vel = jnp.broadcast_to(left_vel, (3, box_count, PAIRS, TILE)).reshape(3, group_size, TILE)
        right_pos = jnp.take(flat_pos, chosen, axis=1)
        right_vel = jnp.take(flat_vel, chosen, axis=1)
        terms = pair_terms(left_pos, left_vel, right_pos, right_vel, noise_block)
        box_force = lax.optimization_barrier(jnp.sum(terms, axis=3)).reshape(3, box_count, PAIRS, TILE).sum(axis=2).reshape(3, box_count * TILE)
        return lax.dynamic_update_slice_in_dim(force, box_force, row_start, 1)
    return lax.fori_loop(0, tiles_here // group_size, add_group, jnp.zeros_like(own_pos))

def contact_forces(mem_pos, mem_vel, flat_pos, flat_vel, mem_vertex, mem_partner, cell_total):
    tiles_here = mem_vertex.shape[0]
    group_size = math.gcd(tiles_here, 16)

    def add_group(loop_turn, carried):
        vertex_force, reaction = carried
        tile_start = (loop_turn * group_size).astype(jnp.int32)
        chosen_vertex = lax.dynamic_slice_in_dim(mem_vertex, tile_start, group_size, 0)
        chosen_partner = lax.dynamic_slice_in_dim(mem_partner, tile_start, group_size, 0)
        left_pos = jnp.take(mem_pos, chosen_vertex, axis=1)
        left_vel = jnp.take(mem_vel, chosen_vertex, axis=1)
        right_pos = jnp.take(flat_pos, chosen_partner, axis=1)
        right_vel = jnp.take(flat_vel, chosen_partner, axis=1)
        alive_mask = (chosen_vertex // V < cell_total).astype(jnp.float32)
        terms = pair_terms(left_pos, left_vel, right_pos, right_vel, 0.0) * alive_mask[None, :, :, None]
        vertex_force = vertex_force.at[:, chosen_vertex.reshape(-1)].add(lax.optimization_barrier(jnp.sum(terms, axis=3)).reshape(3, -1))
        reaction = reaction.at[:, chosen_partner.reshape(-1)].add(-lax.optimization_barrier(jnp.sum(terms, axis=2)).reshape(3, -1))
        return (vertex_force, reaction)
    start_state = (jnp.zeros_like(mem_pos), jnp.zeros_like(flat_pos))
    vertex_force, reaction = lax.fori_loop(0, tiles_here // group_size, add_group, start_state)
    width = (flat_pos.shape[1] - 1) // 9
    reaction = reaction[:, :-1].reshape(3, 3, 3, width).transpose(1, 2, 0, 3)
    return (vertex_force, reaction)

def membrane_forces(mem_pos, bending, rest_size, alive_mask):
    cells_here = rest_size.shape[0]
    shaped = mem_pos.reshape(3, cells_here, V)
    centre = lax.optimization_barrier(jnp.mean(shaped, axis=2, keepdims=True))
    relative = shaped - centre
    bent_once = jnp.einsum('knv,uv->knu', relative, bending, precision=lax.Precision.HIGHEST)
    bent_twice = jnp.einsum('knv,uv->knu', bent_once, bending, precision=lax.Precision.HIGHEST)
    spread = lax.optimization_barrier(jnp.sum(relative * relative, axis=(0, 2))) / V
    stretch = AREA_MODULUS * (spread / rest_size - 1.0)
    internal = -(BENDING_MODULUS * bent_twice + stretch[None, :, None] * relative) * alive_mask[None, :, None]
    return internal.reshape(3, cells_here * V)

def reference(solvent_pos, solvent_vel, pair_index, random_pairs, membrane_pos, membrane_vel, mem_vertex, mem_partner, bending, rest_size, cell_count):
    grid = jnp.concatenate([solvent_pos, solvent_vel], axis=0).reshape(6, N_GX, N_GY, P_DEV).transpose(1, 2, 0, 3)
    tile_grid = pair_index.reshape(BRICKS, TILES_DEV, TILE)
    noise_grid = random_pairs.reshape(BRICKS, TILES_DEV, TILE, TILE)
    mem_grid = membrane_pos.reshape(3, BRICKS, CELL_DEV * V).transpose(1, 0, 2)
    memvel_grid = membrane_vel.reshape(3, BRICKS, CELL_DEV * V).transpose(1, 0, 2)
    vertex_grid = mem_vertex.reshape(BRICKS, MEM_TILES, TILE)
    partner_grid = mem_partner.reshape(BRICKS, MEM_TILES, TILE)

    def one_brick(brick_index):
        row_id = brick_index // N_GY
        col_id = brick_index % N_GY
        row_ids = (row_id + jnp.arange(3, dtype=jnp.int32) - 1) % N_GX
        col_ids = (col_id + jnp.arange(3, dtype=jnp.int32) - 1) % N_GY
        extended = grid[row_ids][:, col_ids]
        flat_pos, flat_vel = neighbourhood(extended)
        own_state = grid[row_id, col_id]
        solvent_force = solvent_forces(own_state[0:3], own_state[3:6], flat_pos, flat_vel, tile_grid[brick_index], noise_grid[brick_index])
        contact, reaction = contact_forces(mem_grid[brick_index], memvel_grid[brick_index], flat_pos, flat_vel, vertex_grid[brick_index], partner_grid[brick_index], cell_count[brick_index])
        return (solvent_force, contact, reaction)
    solvent_force, contact, reaction = lax.map(one_brick, jnp.arange(BRICKS, dtype=jnp.int32))
    reaction = reaction.reshape(N_GX, N_GY, 3, 3, 3, P_DEV)
    returned = jnp.zeros((N_GX, N_GY, 3, P_DEV), jnp.float32)
    for row_step in range(3):
        for col_step in range(3):
            returned = returned + jnp.roll(reaction[:, :, row_step, col_step], (row_step - 1, col_step - 1), axis=(0, 1))
    push = jnp.array([SOLVENT_PUSH, 0.0, 0.0], jnp.float32)[:, None]
    summed = (solvent_force.reshape(N_GX, N_GY, 3, P_DEV) + returned).transpose(2, 0, 1, 3).reshape(3, NP)
    solvent_velocity = solvent_vel + TIME_STEP * (summed + push)
    alive_mask = (jnp.arange(CELL_DEV, dtype=jnp.int32)[None, :] < cell_count[:, None]).reshape(CELLS).astype(jnp.float32)
    internal = membrane_forces(membrane_pos, bending, rest_size, alive_mask)
    contact_all = contact.transpose(1, 0, 2).reshape(3, CELLS * V)
    membrane_velocity = membrane_vel + TIME_STEP * (internal + contact_all)
    return (solvent_velocity, membrane_velocity)
```

```python
import functools
from jax.sharding import PartitionSpec as P
import jax, jax.numpy as jnp
from jax import lax
from jax.experimental import pallas as pl
from jax.experimental.pallas import tpu as pltpu

f32, bf16 = jnp.float32, jnp.bfloat16
BOXES, TILE, PAIRS = 96, 128, 4
GROUP = 8

def split3(v):
    p1 = v.astype(bf16).astype(f32)
    rest = v - p1
    p2 = rest.astype(bf16).astype(f32)
    return p1, p2, rest - p2

NT = (((1,), (1,)), ((), ()))

def row_of(blk):
    return blk + (blk // BOXES) * (5 * BOXES)

def gather_block(tab_ref, blk, low, high, held, row):
    n = blk // BOXES
    dx = ((n // 3) - 1).astype(f32) * 4.0
    dy = ((n % 3) - 1).astype(f32) * 4.0
    block = tab_ref[pl.ds(row_of(blk), 6, stride=BOXES), :]
    got = jnp.take_along_axis(block, low, axis=1, mode="promise_in_bounds")
    got = got + jnp.where(row == 0, dx, jnp.where(row == 1, dy, 0.0))
    return jnp.where(high == blk, got, held)

def solvent_kernel(lo_ref, hi_ref, idx_ref, theta_ref, tab_ref, out_ref, held_ref):
    step = pl.program_id(0)
    tiles = GROUP * PAIRS
    row6 = lax.broadcasted_iota(jnp.int32, (6, TILE), 0)
    row8 = lax.broadcasted_iota(jnp.int32, (8, TILE), 0)
    far = jnp.where(row6 < 3, 1000.0, 0.0)

    @pl.loop(0, tiles // 8)
    def _(part):
        spread = jnp.int32(0)
        for k in range(8):
            t = part * 8 + k
            first = lo_ref[step * tiles + t]
            spread = jnp.maximum(spread, hi_ref[step * tiles + t] - first)
            index = jnp.broadcast_to(idx_ref[pl.ds(t, 1), :], (6, TILE))
            held_ref[t, 0:6, :] = gather_block(tab_ref, first, index & 127, index >> 7, far, row6)

        @pl.when(spread > 0)
        def _():
            @pl.loop(0, 8)
            def _(k):
                t = part * 8 + k
                index = jnp.broadcast_to(idx_ref[pl.ds(t, 1), :], (6, TILE))

                @pl.loop(lo_ref[step * tiles + t] + 1, hi_ref[step * tiles + t] + 1)
                def _(blk):
                    held_ref[t, 0:6, :] = gather_block(tab_ref, blk, index & 127, index >> 7, held_ref[t, 0:6, :], row6)

    @pl.loop(0, GROUP)
    def _(k):
        box = step * GROUP + k
        cx = (box % 2).astype(f32) * 2.0 + 1.0
        cy = (box // 2 % 2).astype(f32) * 2.0 + 1.0
        cz = (box // 4).astype(f32) * 2.0 + 1.0
        centre = jnp.where(row8 == 0, cx, jnp.where(row8 == 1, cy, jnp.where(row8 == 2, cz, 0.0)))
        own = tab_ref[pl.ds(row_of(4 * BOXES + box), 6, stride=BOXES), :] - centre[0:6]
        a, u = own[0:3], own[3:6] * 4.5
        aa = jnp.sum(a * a, axis=0, keepdims=True)
        au = jnp.sum(a * u, axis=0, keepdims=True)
        zero = jnp.zeros((3, TILE), f32)
        one = jnp.ones((1, TILE), f32)
        def left(q, const):
            q1, q2, q3 = split3(q)
            c1, c2, c3 = split3(const)
            last = jnp.where(row8 == 0, c1, jnp.where(row8 == 1, c2, jnp.where(row8 == 2, c3, 0.0)))
            return jnp.concatenate([q1, q1, q1, q2, q2, q3, last, jnp.zeros_like(last)], axis=0)
        ql = left(jnp.concatenate([-2.0 * a, zero, one, 0.0 * one], axis=0), aa)
        qs = left(jnp.concatenate([-u, -4.5 * a, 0.0 * one, 4.5 * one], axis=0), au)
        lhs = jnp.concatenate([ql.T, qs.T], axis=0).astype(bf16)
        vs, ws = [], []
        for j in range(PAIRS):
            held = held_ref[k * PAIRS + j] - centre
            b, w = held[0:3], held[3:6]
            bb = jnp.sum(b * b, axis=0, keepdims=True)
            bw = jnp.sum(b * w, axis=0, keepdims=True)
            full = jnp.where(row8 == 6, bb, jnp.where(row8 == 7, bw, held))
            p1, p2, p3 = split3(full)
            ones = jnp.ones_like(p1)
            vs.append(jnp.concatenate([p1, p2, p3, p1, p2, p1, ones, ones], axis=0).astype(bf16))
            v1 = jnp.where(row8 == 3, 1.0, p1)
            zz = jnp.zeros_like(p1)
            ws.append(jnp.concatenate([v1, jnp.where(row8 < 3, p2, 0.0), jnp.where(row8 < 3, p3, 0.0), zz], axis=0).astype(bf16))
        acc = jnp.zeros((32, TILE), f32)
        for h in range(2):
            rhs = jnp.concatenate(vs[2 * h:2 * h + 2], axis=1)
            out = jnp.dot(lhs, rhs, preferred_element_type=f32)
            r2, s = out[:TILE], out[TILE:]
            th = jnp.concatenate([theta_ref[k * PAIRS + 2 * h], theta_ref[k * PAIRS + 2 * h + 1]], axis=1).astype(f32)
            r2 = jnp.maximum(r2, 1e-12)
            q = lax.rsqrt(r2)
            g = jnp.maximum(jnp.minimum(q, 10.0) * (1.0 - r2 * q), 0.0)
            force = g * (25.0 + 30.0 * th - g * s)
            fh = force.astype(bf16)
            fl = (force - fh.astype(f32)).astype(bf16)
            wv = jnp.concatenate(ws[2 * h:2 * h + 2], axis=1)
            acc += lax.dot_general(wv, fh, NT, preferred_element_type=f32)
            acc += lax.dot_general(wv, fl, NT, preferred_element_type=f32)
        total = acc[0:8] + acc[8:16] + acc[16:24]
        res = a * acc[3:4] - total[0:3]
        out_ref[:, pl.ds(k, 1), :] = res[:, None, :]

def solvent(tab, idx, theta):
    tiles = idx.shape[0]
    hi = idx >> 7
    full = idx >= 9 * BOXES * TILE
    first = jnp.min(jnp.where(full, 9 * BOXES - 1, hi), axis=1)
    last = jnp.max(jnp.where(full, 0, hi), axis=1)
    last = jnp.maximum(first, last)
    return pl.pallas_call(
        solvent_kernel,
        out_shape=jax.ShapeDtypeStruct((3, BOXES, TILE), f32),
        grid=(BOXES // GROUP,),
        in_specs=[
            pl.BlockSpec(memory_space=pltpu.SMEM),
            pl.BlockSpec(memory_space=pltpu.SMEM),
            pl.BlockSpec((GROUP * PAIRS, TILE), lambda i: (i, 0)),
            pl.BlockSpec((GROUP * PAIRS, TILE, TILE), lambda i: (i, 0, 0)),
            pl.BlockSpec((9 * 6 * BOXES, TILE), lambda i: (0, 0), pipeline_mode=pl.Buffered(1)),
        ],
        out_specs=pl.BlockSpec((3, GROUP, TILE), lambda i: (0, i, 0)),
        scratch_shapes=[pltpu.VMEM((GROUP * PAIRS, 8, TILE), f32)],
        compiler_params=pltpu.CompilerParams(vmem_limit_bytes=40 * 2**20),
        cost_estimate=pl.CostEstimate(flops=10**10, bytes_accessed=2 * 10**7, transcendentals=0),
        name="solvent",
    )(first, last, idx, theta, tab.reshape(9 * 6 * BOXES, TILE))


V = 642
MEM_TILES = 64
MB = 96
WIN = 8
SPAN = 16

def gather_window(tab_ref, base, low, high, held):
    for k in range(WIN):
        block = tab_ref[pl.ds(base + k, 6, stride=MB), :]
        got = jnp.take_along_axis(block, low, axis=1, mode="promise_in_bounds")
        held = jnp.where(high == base + k, got, held)
    return held

def scatter_vertex(con_ref, base, low, high, pieces, rowt, row16):
    onehot = (rowt == low).astype(f32).astype(bf16)
    hit = high == row16 + base
    left = jnp.concatenate([jnp.where(hit, p[c:c + 1], 0.0) for p in pieces for c in range(3)], axis=0).astype(bf16)
    out = lax.dot_general(left, onehot, NT, preferred_element_type=f32)
    out = out[:3 * SPAN] + out[3 * SPAN:]
    for c in range(3):
        con_ref[c, pl.ds(base, SPAN), :] += out[c * SPAN:(c + 1) * SPAN]

def scatter_partner(rea_ref, blk, low, high, pieces, rowt):
    onehot = ((rowt == low) & (high == blk)).astype(f32).astype(bf16)
    out = lax.dot_general(pieces, onehot, NT, preferred_element_type=f32)
    out = (out[0:8] + out[8:16])[0:3]
    rea_ref[pl.ds(blk + (blk // BOXES) * (2 * BOXES), 3, stride=BOXES), :] += out

def contact_kernel(plo, phi, vlo, vhi, count, par_ref, ver_ref, tab_ref, mem_ref, con_ref, rea_ref, lh_ref, rh_ref, fo_ref):
    row6 = lax.broadcasted_iota(jnp.int32, (6, TILE), 0)
    row8 = lax.broadcasted_iota(jnp.int32, (8, TILE), 0)
    rowt = lax.broadcasted_iota(jnp.int32, (TILE, TILE), 0)
    row16 = lax.broadcasted_iota(jnp.int32, (SPAN, TILE), 0)
    far = jnp.where(row6 < 3, 1000.0, 0.0)
    alive_end = count[0] * V
    con_ref[...] = jnp.zeros_like(con_ref)
    rea_ref[...] = jnp.zeros_like(rea_ref)

    @pl.loop(0, MEM_TILES // 8)
    def _(part):
        spread = jnp.int32(0)
        vspread = jnp.int32(0)
        for k in range(8):
            t = part * 8 + k
            first = plo[t]
            spread = jnp.maximum(spread, phi[t] - first)
            vspread = jnp.maximum(vspread, vhi[t] - vlo[t])
            index = jnp.broadcast_to(par_ref[pl.ds(t, 1), :], (6, TILE))
            rh_ref[t, 0:6, :] = gather_block(tab_ref, first, index & 127, index >> 7, far, row6)
            vert = jnp.broadcast_to(ver_ref[pl.ds(t, 1), :], (6, TILE))
            high = jnp.where(vert < alive_end, vert >> 7, -1)
            lh_ref[t, 0:6, :] = gather_window(mem_ref, vlo[t], vert & 127, high, far)

        @pl.when(spread > 0)
        def _():
            @pl.loop(0, 8)
            def _(k):
                t = part * 8 + k
                index = jnp.broadcast_to(par_ref[pl.ds(t, 1), :], (6, TILE))

                @pl.loop(plo[t] + 1, phi[t] + 1)
                def _(blk):
                    rh_ref[t, 0:6, :] = gather_block(tab_ref, blk, index & 127, index >> 7, rh_ref[t, 0:6, :], row6)

        @pl.when(vspread >= WIN)
        def _():
            @pl.loop(0, 8)
            def _(k):
                t = part * 8 + k
                vert = jnp.broadcast_to(ver_ref[pl.ds(t, 1), :], (6, TILE))
                high = jnp.where(vert < alive_end, vert >> 7, -1)

                @pl.loop(1, (vhi[t] - vlo[t]) // WIN + 1)
                def _(j):
                    lh_ref[t, 0:6, :] = gather_window(mem_ref, vlo[t] + j * WIN, vert & 127, high, lh_ref[t, 0:6, :])

    unit = [jnp.where(row8 == c, 1.0, 0.0) for c in range(6)]
    scale = jnp.where(row8 < 3, 1.0, 4.5)

    @pl.loop(0, MEM_TILES)
    def _(t):
        blk = plo[t]
        n, box = blk // BOXES, blk % BOXES
        cx = (n // 3 - 1).astype(f32) * 4.0 + (box % 2).astype(f32) * 2.0 + 1.0
        cy = (n % 3 - 1).astype(f32) * 4.0 + (box // 2 % 2).astype(f32) * 2.0 + 1.0
        cz = (box // 4).astype(f32) * 2.0 + 1.0
        centre = jnp.where(row8 == 0, cx, jnp.where(row8 == 1, cy, jnp.where(row8 == 2, cz, 0.0)))
        live6 = row8 < 6
        lv = jnp.where(live6, lh_ref[t] - centre, 0.0)
        rv = jnp.where(live6, rh_ref[t] - centre, 0.0)
        a1, a2, a3 = split3(lv * scale)
        b1, b2, b3 = split3(rv * scale)
        one = jnp.ones_like(a1)
        zero = jnp.zeros_like(a1)
        left = jnp.concatenate([a1, a2, a3, one, one, one], axis=0).T.astype(bf16)
        diffs = []
        for c in range(6):
            rhs = jnp.concatenate([unit[c], unit[c], unit[c], -b1 * unit[c], -b2 * unit[c], -b3 * unit[c]], axis=0).astype(bf16)
            diffs.append(jnp.dot(left, rhs, preferred_element_type=f32))
        dx, dy, dz, du, dv, dw = diffs
        r2 = dx * dx + dy * dy + dz * dz
        s = dx * du + dy * dv + dz * dw
        r2 = jnp.maximum(r2, 1e-12)
        q = lax.rsqrt(r2)
        g = jnp.maximum(jnp.minimum(q, 10.0) * (1.0 - r2 * q), 0.0)
        force = g * (25.0 - g * s)
        fh = force.astype(bf16)
        fl = (force - fh.astype(f32)).astype(bf16)
        def sums(p1, p2, p3):
            one3 = jnp.where(row8 == 3, 1.0, jnp.where(row8 < 3, p1, 0.0))
            return jnp.concatenate([one3, jnp.where(row8 < 3, p2, 0.0), jnp.where(row8 < 3, p3, 0.0), zero], axis=0).astype(bf16)
        wb, wa = sums(b1, b2, b3), sums(a1, a2, a3)
        oc = lax.dot_general(wb, fh, NT, preferred_element_type=f32) + lax.dot_general(wb, fl, NT, preferred_element_type=f32)
        orr = jnp.dot(wa, fh, preferred_element_type=f32) + jnp.dot(wa, fl, preferred_element_type=f32)
        oc = oc[0:8] + oc[8:16] + oc[16:24]
        orr = orr[0:8] + orr[8:16] + orr[16:24]
        fo_ref[t, 0:8, :] = lv * oc[3:4] - oc
        fo_ref[t, 8:16, :] = rv * orr[3:4] - orr

    @pl.loop(0, MEM_TILES // 4)
    def _(part):
        for k in range(4):
            t = part * 4 + k
            con, rea = fo_ref[t, 0:8, :], fo_ref[t, 8:16, :]
            c1 = con.astype(bf16).astype(f32)
            vert = ver_ref[pl.ds(t, 1), :]
            base = pl.multiple_of(vlo[t] // 8 * 8, 8)
            scatter_vertex(con_ref, base, vert & 127, vert >> 7, (c1, con - c1), rowt, row16)

            @pl.loop(1, (vhi[t] - base) // SPAN + 1)
            def _(j):
                scatter_vertex(con_ref, pl.multiple_of(base + j * SPAN, 8), vert & 127, vert >> 7, (c1, con - c1), rowt, row16)

            rea = jnp.where(row8 < 3, rea, 0.0)
            r1 = rea.astype(bf16).astype(f32)
            pieces = jnp.concatenate([r1, rea - r1], axis=0).astype(bf16)
            index = par_ref[pl.ds(t, 1), :]
            scatter_partner(rea_ref, plo[t], index & 127, index >> 7, pieces, rowt)

            @pl.loop(plo[t] + 1, phi[t] + 1)
            def _(blk):
                scatter_partner(rea_ref, blk, index & 127, index >> 7, pieces, rowt)

def contact(tab, mpos, mvel, vertex, partner, count):
    mem = jnp.concatenate([mpos, mvel], axis=0)
    mem = jnp.pad(mem, ((0, 0), (0, MB * TILE - mem.shape[1]))).reshape(6 * MB, TILE)
    smem = pl.BlockSpec(memory_space=pltpu.SMEM)
    vmem = pl.BlockSpec(memory_space=pltpu.VMEM)
    con, rea = pl.pallas_call(
        contact_kernel,
        out_shape=(jax.ShapeDtypeStruct((3, MB, TILE), f32), jax.ShapeDtypeStruct((3 * 9 * BOXES, TILE), f32)),
        in_specs=[smem] * 5 + [vmem] * 4,
        out_specs=(vmem, vmem),
        scratch_shapes=[pltpu.VMEM((MEM_TILES, 8, TILE), f32), pltpu.VMEM((MEM_TILES, 8, TILE), f32), pltpu.VMEM((MEM_TILES, 16, TILE), f32)],
        compiler_params=pltpu.CompilerParams(vmem_limit_bytes=40 * 2**20),
        name="contact",
    )(jnp.min(partner, 1) >> 7, jnp.max(partner, 1) >> 7, jnp.min(vertex, 1) >> 7, jnp.max(vertex, 1) >> 7, count,
      partner, vertex, tab.reshape(9 * 6 * BOXES, TILE), mem)
    return con, rea.reshape(9, 3, BOXES, TILE)

TIME_STEP = 0.01
BENDING_MODULUS = 20.0
AREA_MODULUS = 40.0
SOLVENT_PUSH = 0.5

def moved(array, by_x, by_y):
    nx, ny = lax.axis_size("gx"), lax.axis_size("gy")
    pairs = [(i * ny + j, (i + by_x) % nx * ny + (j + by_y) % ny) for i in range(nx) for j in range(ny)]
    return lax.ppermute(array, ("gx", "gy"), pairs)

def membrane_forces(mem_pos, bending, rest_size, alive_mask):
    cells_here = rest_size.shape[0]
    shaped = mem_pos.reshape(3, cells_here, V)
    centre = jnp.mean(shaped, axis=2, keepdims=True)
    relative = shaped - centre
    bent_once = jnp.einsum("knv,uv->knu", relative, bending, precision=lax.Precision.HIGHEST)
    bent_twice = jnp.einsum("knv,uv->knu", bent_once, bending, precision=lax.Precision.HIGHEST)
    spread = jnp.sum(relative * relative, axis=(0, 2)) / V
    stretch = AREA_MODULUS * (spread / rest_size - 1.0)
    internal = -(BENDING_MODULUS * bent_twice + stretch[None, :, None] * relative) * alive_mask[None, :, None]
    return internal.reshape(3, cells_here * V)

def on_device(solvent_pos, solvent_vel, pair_index, random_pairs, membrane_pos, membrane_vel, mem_vertex, mem_partner,
              bending, rest_size, cell_count):
    vel = solvent_vel.reshape(3, BOXES, TILE)
    own = jnp.concatenate([solvent_pos.reshape(3, BOXES, TILE), vel], axis=0)[None]
    column = jnp.concatenate([moved(own, 0, 1), own, moved(own, 0, -1)], axis=0)
    tab = jnp.concatenate([moved(column, 1, 0), column, moved(column, -1, 0)], axis=0)
    alive_mask = (jnp.arange(rest_size.shape[0], dtype=jnp.int32) < cell_count[0]).astype(f32)
    internal = membrane_forces(membrane_pos, bending, rest_size, alive_mask)
    con, rea = contact(tab, membrane_pos, membrane_vel, mem_vertex, mem_partner, cell_count)
    back = [rea[3 * p + q] if (p, q) == (1, 1) else moved(rea[3 * p + q], p - 1, q - 1) for p in range(3) for q in range(3)]
    force = solvent(tab, pair_index, random_pairs)
    returned = sum(back[1:], back[0])
    push = jnp.array([SOLVENT_PUSH, 0.0, 0.0], f32)[:, None, None]
    solvent_velocity = (vel + TIME_STEP * (force + returned + push)).reshape(3, BOXES * TILE)
    touch = con.reshape(3, MB * TILE)[:, :membrane_pos.shape[1]]
    membrane_velocity = membrane_vel + TIME_STEP * (internal + touch)
    return solvent_velocity, membrane_velocity

def solution(mesh):
    both = ("gx", "gy")
    flat, tiles = P(None, both), P(both, None)
    return jax.shard_map(
        on_device,
        mesh=mesh,
        in_specs=(flat, flat, tiles, P(both, None, None), flat, flat, tiles, tiles, P(), P(both), P(both)),
        out_specs=(flat, flat),
        check_vma=False,
    )
```

```python
import functools
from jax.sharding import PartitionSpec as P
import jax, jax.numpy as jnp
from jax import lax
from jax.experimental import pallas as pl
from jax.experimental.pallas import tpu as pltpu

f32, bf16 = jnp.float32, jnp.bfloat16
BOXES, TILE, PAIRS = 96, 128, 4
GROUP = 8
AHEAD = 1

def split3(v):
    p1 = v.astype(bf16).astype(f32)
    rest = v - p1
    p2 = rest.astype(bf16).astype(f32)
    return p1, p2, rest - p2

NT = (((1,), (1,)), ((), ()))

def part_of(blk):
    return (blk * 683) >> 16

def row_of(blk):
    return blk + part_of(blk) * (5 * BOXES)

def gather_block(tab_ref, blk, low, high, held, row):
    n = part_of(blk)
    p = (n * 11) >> 5
    dx = (p - 1).astype(f32) * 4.0
    dy = (n - 3 * p - 1).astype(f32) * 4.0
    block = tab_ref[pl.ds(blk + n * (5 * BOXES), 6, stride=BOXES), :]
    got = jnp.take_along_axis(block, low, axis=1, mode="promise_in_bounds")
    got = got + jnp.where(row == 0, dx, jnp.where(row == 1, dy, 0.0))
    return jnp.where(high == blk, got, held)

def box_centre(box, row8):
    cx = (box & 1).astype(f32) * 2.0 + 1.0
    cy = ((box >> 1) & 1).astype(f32) * 2.0 + 1.0
    cz = (box >> 2).astype(f32) * 2.0 + 1.0
    return jnp.where(row8 == 0, cx, jnp.where(row8 == 1, cy, jnp.where(row8 == 2, cz, 0.0)))

def own_features(own, row8):
    a, u = own[0:3], own[3:6] * 4.5
    aa = jnp.sum(a * a, axis=0, keepdims=True)
    au = jnp.sum(a * u, axis=0, keepdims=True)
    zero = jnp.zeros((3, TILE), f32)
    one = jnp.ones((1, TILE), f32)
    def left(q, const):
        q1, q2, q3 = split3(q)
        c1, c2, c3 = split3(const)
        last = jnp.where(row8 == 0, c1, jnp.where(row8 == 1, c2, jnp.where(row8 == 2, c3, 0.0)))
        return jnp.concatenate([q1, q1, q1, q2, q2, q3, last, jnp.zeros_like(last)], axis=0)
    ql = left(jnp.concatenate([-2.0 * a, zero, one, 0.0 * one], axis=0), aa)
    qs = left(jnp.concatenate([-u, -4.5 * a, 0.0 * one, 4.5 * one], axis=0), au)
    return jnp.concatenate([ql.T, qs.T], axis=0).astype(bf16)

def right_features(held, centre, row8):
    held = jnp.concatenate([held, held[0:2]], axis=0) - centre
    b, w = held[0:3], held[3:6]
    bb = jnp.sum(b * b, axis=0, keepdims=True)
    bw = jnp.sum(b * w, axis=0, keepdims=True)
    full = jnp.where(row8 == 6, bb, jnp.where(row8 == 7, bw, held))
    p1, p2, p3 = split3(full)
    ones = jnp.ones_like(p1)
    v1 = jnp.where(row8 == 3, 1.0, p1)
    return (jnp.concatenate([p1, p2, p3, p1, p2, p1, ones, ones], axis=0).astype(bf16),
            jnp.concatenate([v1, p2, p3, p3], axis=0).astype(bf16))

def pair_force(out, theta_ref, k, h):
    r2, s = out[:TILE], out[TILE:]
    th = jnp.concatenate([theta_ref[k * PAIRS + 2 * h], theta_ref[k * PAIRS + 2 * h + 1]], axis=1).astype(f32)
    r2 = jnp.maximum(r2, 1e-12)
    q = lax.rsqrt(r2)
    g = jnp.maximum(jnp.minimum(q, 10.0) * (1.0 - r2 * q), 0.0)
    force = g * (25.0 + 30.0 * th - g * s)
    fh = force.astype(bf16)
    return fh, (force - fh.astype(f32)).astype(bf16)

def solvent_kernel(lo_ref, hi_ref, idx_ref, theta1_ref, theta2_ref, tab_ref, out_ref, *held_refs):
    step = pl.program_id(0)
    steps = BOXES // GROUP // 2
    tiles = GROUP * PAIRS
    row6 = lax.broadcasted_iota(jnp.int32, (6, TILE), 0)
    row8 = lax.broadcasted_iota(jnp.int32, (8, TILE), 0)
    far = jnp.where(row6 < 3, 1000.0, 0.0)
    even, odd = held_refs[:3], held_refs[3:]

    def section(group, row, made, used, before, theta_ref):
        lhs_ref, rhs_ref, sum_ref = made
        spread = jnp.int32(0)
        products, forces = {}, {}

        def product(unit):
            k, h = divmod(unit, 2)
            at = pl.ds(h * 2 * TILE, 2 * TILE)
            products[unit] = jnp.dot(used[0][k], used[1][k, :, at], preferred_element_type=f32)

        def finish(k):
            acc = jnp.zeros((32, TILE), f32)
            for h in range(2):
                sums = used[2][k, :, pl.ds(h * 2 * TILE, 2 * TILE)]
                for force in forces.pop(2 * k + h):
                    acc += lax.dot_general(sums, force, NT, preferred_element_type=f32)
            total = acc[0:8] + acc[8:16] + acc[16:24]
            last = before * GROUP + k
            a = tab_ref[pl.ds(4 * 6 * BOXES + last, 6, stride=BOXES), :] - box_centre(last, row8)[0:6]
            out_ref[:, pl.ds(last, 1), :] = (a[0:3] * acc[3:4] - total[0:3])[:, None, :]

        for ahead in range(AHEAD):
            product(ahead)
        for k in range(GROUP):
            for h in range(2):
                unit = 2 * k + h
                if unit + AHEAD < 2 * GROUP:
                    product(unit + AHEAD)
                forces[unit] = pair_force(products.pop(unit), theta_ref, k, h)
            if k > 0:
                finish(k - 1)

            box = group * GROUP + k
            centre = box_centre(box, row8)
            own = tab_ref[pl.ds(4 * 6 * BOXES + box, 6, stride=BOXES), :]
            lhs_ref[k] = own_features(own - centre[0:6], row8)
            for j in range(PAIRS):
                t = k * PAIRS + j
                first = lo_ref[group * tiles + t]
                spread = jnp.maximum(spread, hi_ref[group * tiles + t] - first)
                index = jnp.broadcast_to(idx_ref[pl.ds(row + t, 1), :], (6, TILE))
                held = gather_block(tab_ref, first, index & 127, index >> 7, far, row6)
                at = pl.ds(j * TILE, TILE)
                rhs_ref[k, :, at], sum_ref[k, :, at] = right_features(held, centre, row8)
        finish(GROUP - 1)

        @pl.when(spread > 0)
        def _():
            for j in range(PAIRS):
                @pl.loop(0, GROUP)
                def _(k):
                    t = k * PAIRS + j
                    index = jnp.broadcast_to(idx_ref[pl.ds(row + t, 1), :], (6, TILE))
                    held = lax.fori_loop(
                        lo_ref[group * tiles + t], hi_ref[group * tiles + t] + 1,
                        lambda blk, held: gather_block(tab_ref, blk, index & 127, index >> 7, held, row6), far)
                    at = pl.ds(j * TILE, TILE)
                    rhs_ref[k, :, at], sum_ref[k, :, at] = right_features(held, box_centre(group * GROUP + k, row8), row8)

    @pl.when(step == 0)
    def _():
        for ref in odd:
            ref[...] = jnp.zeros_like(ref)

    section(jnp.minimum(step, steps - 1) * 2, 0, even, odd, jnp.maximum(2 * step - 1, 0), theta1_ref)

    @pl.when(step < steps)
    def _():
        section(step * 2 + 1, tiles, odd, even, step * 2, theta2_ref)

def solvent(tab, idx, theta):
    hi = idx >> 7
    full = idx >= 9 * BOXES * TILE
    first = jnp.min(jnp.where(full, 9 * BOXES - 1, hi), axis=1)
    last = jnp.max(jnp.where(full, 0, hi), axis=1)
    last = jnp.maximum(first, last)
    steps = BOXES // GROUP // 2
    return pl.pallas_call(
        solvent_kernel,
        out_shape=jax.ShapeDtypeStruct((3, BOXES, TILE), f32),
        grid=(BOXES // GROUP // 2 + 1,),
        in_specs=[
            pl.BlockSpec(memory_space=pltpu.SMEM),
            pl.BlockSpec(memory_space=pltpu.SMEM),
            pl.BlockSpec((2 * GROUP * PAIRS, TILE), lambda i: (jnp.minimum(i, steps - 1), 0)),
            pl.BlockSpec((GROUP * PAIRS, TILE, TILE), lambda i: (jnp.maximum(2 * i - 1, 0), 0, 0)),
            pl.BlockSpec((GROUP * PAIRS, TILE, TILE), lambda i: (jnp.minimum(2 * i, 2 * steps - 2), 0, 0)),
            pl.BlockSpec((9 * 6 * BOXES, TILE), lambda i: (0, 0), pipeline_mode=pl.Buffered(1)),
        ],
        out_specs=pl.BlockSpec((3, BOXES, TILE), lambda i: (0, 0, 0)),
        scratch_shapes=[pltpu.VMEM((GROUP, 256, 64), bf16), pltpu.VMEM((GROUP, 64, 512), bf16), pltpu.VMEM((GROUP, 32, 512), bf16)] * 2,
        compiler_params=pltpu.CompilerParams(vmem_limit_bytes=40 * 2**20),
        cost_estimate=pl.CostEstimate(flops=10**10, bytes_accessed=2 * 10**7, transcendentals=0),
        name="solvent",
    )(first, last, idx, theta, theta, tab.reshape(9 * 6 * BOXES, TILE))


V = 642
MEM_TILES = 64
MB = 96
WIN = 8
SPAN = 16
UNG, UNC, UNS = 16, 8, 16

def gather_window(tab_ref, base, low, high, held):
    for k in range(WIN):
        block = tab_ref[pl.ds(base + k, 6, stride=MB), :]
        got = jnp.take_along_axis(block, low, axis=1, mode="promise_in_bounds")
        held = jnp.where(high == base + k, got, held)
    return held

def vertex_sums(base, low, high, pieces, rowt, row16):
    onehot = (rowt == low).astype(f32).astype(bf16)
    hit = high == row16 + base
    left = jnp.concatenate([jnp.where(hit, p[c:c + 1], 0.0) for p in pieces for c in range(3)], axis=0).astype(bf16)
    out = lax.dot_general(left, onehot, NT, preferred_element_type=f32)
    return out[:3 * SPAN] + out[3 * SPAN:]

def add_vertex(con_ref, base, out):
    for c in range(3):
        con_ref[c, pl.ds(base, SPAN), :] += out[c * SPAN:(c + 1) * SPAN]

def partner_sums(blk, low, high, pieces, rowt):
    onehot = ((rowt == low) & (high == blk)).astype(f32).astype(bf16)
    out = lax.dot_general(pieces, onehot, NT, preferred_element_type=f32)
    return (out[0:8] + out[8:16])[0:3]

def add_partner(rea_ref, blk, out):
    rea_ref[pl.ds(blk + part_of(blk) * (2 * BOXES), 3, stride=BOXES), :] += out

def contact_kernel(plo, phi, vlo, vhi, count, par_ref, ver_ref, tab_ref, mem_ref, con_ref, rea_ref, lh_ref, rh_ref, fo_ref):
    row6 = lax.broadcasted_iota(jnp.int32, (6, TILE), 0)
    row8 = lax.broadcasted_iota(jnp.int32, (8, TILE), 0)
    rowt = lax.broadcasted_iota(jnp.int32, (TILE, TILE), 0)
    row16 = lax.broadcasted_iota(jnp.int32, (SPAN, TILE), 0)
    far = jnp.where(row6 < 3, 1000.0, 0.0)
    alive_end = count[0] * V
    con_ref[...] = jnp.zeros_like(con_ref)
    rea_ref[...] = jnp.zeros_like(rea_ref)

    @pl.loop(0, MEM_TILES // UNG)
    def _(part):
        spread = jnp.int32(0)
        vspread = jnp.int32(0)
        for k in range(UNG):
            t = part * UNG + k
            first = plo[t]
            spread = jnp.maximum(spread, phi[t] - first)
            vspread = jnp.maximum(vspread, vhi[t] - vlo[t])
            index = jnp.broadcast_to(par_ref[pl.ds(t, 1), :], (6, TILE))
            rh_ref[t, 0:6, :] = gather_block(tab_ref, first, index & 127, index >> 7, far, row6)
            vert = jnp.broadcast_to(ver_ref[pl.ds(t, 1), :], (6, TILE))
            high = jnp.where(vert < alive_end, vert >> 7, -1)
            lh_ref[t, 0:6, :] = gather_window(mem_ref, vlo[t], vert & 127, high, far)

        @pl.when(spread > 0)
        def _():
            @pl.loop(0, UNG)
            def _(k):
                t = part * UNG + k
                index = jnp.broadcast_to(par_ref[pl.ds(t, 1), :], (6, TILE))

                @pl.loop(plo[t] + 1, phi[t] + 1)
                def _(blk):
                    rh_ref[t, 0:6, :] = gather_block(tab_ref, blk, index & 127, index >> 7, rh_ref[t, 0:6, :], row6)

        @pl.when(vspread >= WIN)
        def _():
            @pl.loop(0, UNG)
            def _(k):
                t = part * UNG + k
                vert = jnp.broadcast_to(ver_ref[pl.ds(t, 1), :], (6, TILE))
                high = jnp.where(vert < alive_end, vert >> 7, -1)

                @pl.loop(1, (vhi[t] - vlo[t]) // WIN + 1)
                def _(j):
                    lh_ref[t, 0:6, :] = gather_window(mem_ref, vlo[t] + j * WIN, vert & 127, high, lh_ref[t, 0:6, :])

    def centre_of(blk):
        n = part_of(blk)
        box = blk - BOXES * n
        p = (n * 11) >> 5
        cx = ((p - 1) * 4 + (box & 1) * 2 + 1).astype(f32)
        cy = ((n - 3 * p - 1) * 4 + ((box >> 1) & 1) * 2 + 1).astype(f32)
        cz = ((box >> 2) * 2 + 1).astype(f32)
        return jnp.where(row8 == 0, cx, jnp.where(row8 == 1, cy, jnp.where(row8 == 2, cz, 0.0)))

    def store_forces(t, r2, s, centre, wa, wb):
        r2 = jnp.maximum(r2, 1e-12)
        q = lax.rsqrt(r2)
        g = jnp.maximum(jnp.minimum(q, 10.0) * (1.0 - r2 * q), 0.0)
        force = g * (25.0 - g * s)
        fh = force.astype(bf16)
        fl = (force - fh.astype(f32)).astype(bf16)
        con = lax.dot_general(wb, fh, NT, preferred_element_type=f32) + lax.dot_general(wb, fl, NT, preferred_element_type=f32)
        rea = jnp.dot(wa, fh, preferred_element_type=f32) + jnp.dot(wa, fl, preferred_element_type=f32)
        fo_ref[t, 0:8, :] = (lh_ref[t] - centre) * con[3:4] - (con[0:8] + con[8:16] + con[16:24])
        fo_ref[t, 8:16, :] = (rh_ref[t] - centre) * rea[3:4] - (rea[0:8] + rea[8:16] + rea[16:24])

    unit = [jnp.where(row8 == c, 1.0, 0.0) for c in range(6)]
    scale = jnp.where(row8 < 3, 1.0, 4.5)

    @pl.loop(0, MEM_TILES // UNC)
    def _(part):
        spread = jnp.int32(0)
        for k in range(UNC):
            t = part * UNC + k
            spread = jnp.maximum(spread, phi[t] - plo[t])
            centre = centre_of(plo[t])
            left, right = lh_ref[t, 0:6, :], rh_ref[t, 0:6, :]
            lhs = own_features(left - centre[0:6], row8)
            rhs, wb = right_features(right, centre, row8)
            wa = right_features(left, centre, row8)[1]
            out = jnp.dot(lhs, rhs, preferred_element_type=f32)
            store_forces(t, out[:TILE], out[TILE:], centre, wa, wb)

        @pl.when(spread > 0)
        def _():
            @pl.loop(0, UNC)
            def _(k):
                t = part * UNC + k
                centre = centre_of(plo[t])
                left, right = lh_ref[t, 0:6, :], rh_ref[t, 0:6, :]
                wb, wa = right_features(right, centre, row8)[1], right_features(left, centre, row8)[1]
                live6 = row8 < 6
                a1, a2, a3 = split3(jnp.where(live6, lh_ref[t] - centre, 0.0) * scale)
                b1, b2, b3 = split3(jnp.where(live6, rh_ref[t] - centre, 0.0) * scale)
                one = jnp.ones_like(a1)
                left = jnp.concatenate([a1, a2, a3, one, one, one], axis=0).T.astype(bf16)
                diffs = []
                for c in range(6):
                    rhs = jnp.concatenate([unit[c], unit[c], unit[c], -b1 * unit[c], -b2 * unit[c], -b3 * unit[c]], axis=0).astype(bf16)
                    diffs.append(jnp.dot(left, rhs, preferred_element_type=f32))
                dx, dy, dz, du, dv, dw = diffs
                store_forces(t, dx * dx + dy * dy + dz * dz, dx * du + dy * dv + dz * dw, centre, wa, wb)

    def pieces_of(t):
        con, rea = fo_ref[t, 0:8, :], jnp.where(row8 < 3, fo_ref[t, 8:16, :], 0.0)
        c1 = con.astype(bf16).astype(f32)
        r1 = rea.astype(bf16).astype(f32)
        return (c1, con - c1), jnp.concatenate([r1, rea - r1], axis=0).astype(bf16)

    @pl.loop(0, MEM_TILES // UNS)
    def _(part):
        more = jnp.int32(0)
        sums = []
        for k in range(UNS):
            t = part * UNS + k
            con, rea = pieces_of(t)
            vert, index = ver_ref[pl.ds(t, 1), :], par_ref[pl.ds(t, 1), :]
            base = pl.multiple_of((vlo[t] >> 3) << 3, 8)
            more = jnp.maximum(more, jnp.maximum(phi[t] - plo[t], (vhi[t] - base) >> 4))
            sums.append((base, vertex_sums(base, vert & 127, vert >> 7, con, rowt, row16),
                         plo[t], partner_sums(plo[t], index & 127, index >> 7, rea, rowt)))
        for base, con, blk, rea in sums:
            add_vertex(con_ref, base, con)
            add_partner(rea_ref, blk, rea)

        @pl.when(more > 0)
        def _():
            @pl.loop(0, UNS)
            def _(k):
                t = part * UNS + k
                con, rea = pieces_of(t)
                vert, index = ver_ref[pl.ds(t, 1), :], par_ref[pl.ds(t, 1), :]
                base = (vlo[t] >> 3) << 3

                @pl.loop(1, ((vhi[t] - base) >> 4) + 1)
                def _(j):
                    at = pl.multiple_of(base + j * SPAN, 8)
                    add_vertex(con_ref, at, vertex_sums(at, vert & 127, vert >> 7, con, rowt, row16))

                @pl.loop(plo[t] + 1, phi[t] + 1)
                def _(blk):
                    add_partner(rea_ref, blk, partner_sums(blk, index & 127, index >> 7, rea, rowt))

def contact(tab, mpos, mvel, vertex, partner, count):
    mem = jnp.concatenate([mpos, mvel], axis=0)
    mem = jnp.pad(mem, ((0, 0), (0, MB * TILE - mem.shape[1]))).reshape(6 * MB, TILE)
    smem = pl.BlockSpec(memory_space=pltpu.SMEM)
    vmem = pl.BlockSpec(memory_space=pltpu.VMEM)
    con, rea = pl.pallas_call(
        contact_kernel,
        out_shape=(jax.ShapeDtypeStruct((3, MB, TILE), f32), jax.ShapeDtypeStruct((3 * 9 * BOXES, TILE), f32)),
        in_specs=[smem] * 5 + [vmem] * 4,
        out_specs=(vmem, vmem),
        scratch_shapes=[pltpu.VMEM((MEM_TILES, 8, TILE), f32), pltpu.VMEM((MEM_TILES, 8, TILE), f32), pltpu.VMEM((MEM_TILES, 16, TILE), f32)],
        compiler_params=pltpu.CompilerParams(vmem_limit_bytes=40 * 2**20),
        name="contact",
    )(jnp.min(partner, 1) >> 7, jnp.max(partner, 1) >> 7, jnp.min(vertex, 1) >> 7, jnp.max(vertex, 1) >> 7, count,
      partner, vertex, tab.reshape(9 * 6 * BOXES, TILE), mem)
    return con, rea.reshape(9, 3, BOXES, TILE)

TIME_STEP = 0.01
BENDING_MODULUS = 20.0
AREA_MODULUS = 40.0
SOLVENT_PUSH = 0.5

MESH = pl.DeviceIdType.MESH
CHUNKS = 3

def halo_kernel(nx, ny, own_ref, x_ref, bend_ref, cell_ref, tab_ref, internal_ref, send_sem, recv_sem, own_sem):
    gx, gy = lax.axis_index("gx"), lax.axis_index("gy")
    up, down = (lax.rem(gx + 1, nx), gy), (lax.rem(gx + nx - 1, nx), gy)
    right, left = (gx, lax.rem(gy + 1, ny)), (gx, lax.rem(gy + ny - 1, ny))
    size = own_ref.shape[0]
    part = size // CHUNKS

    barrier = pltpu.get_barrier_semaphore()
    for device in (up, down, right, left):
        pl.semaphore_signal(barrier, inc=1, device_id=device, device_id_type=MESH)
    pl.semaphore_wait(barrier, 4)

    def slot(n, c):
        return tab_ref.at[pl.ds(n * size + c * part, part)]

    def copy(source, n, c, device):
        src = own_ref.at[pl.ds(c * part, part)] if source is None else slot(source, c)
        return pltpu.make_async_remote_copy(
            src_ref=src, dst_ref=slot(n, c), send_sem=send_sem.at[n, c], recv_sem=recv_sem.at[n, c],
            device_id=device, device_id_type=MESH)

    keep = pltpu.make_async_copy(own_ref, tab_ref.at[pl.ds(4 * size, size)], own_sem)
    keep.start()
    first = [[copy(None, 3, c, right), copy(None, 5, c, left)] for c in range(CHUNKS)]
    along = [[copy(None, 1, c, up), copy(None, 7, c, down)] for c in range(CHUNKS)]
    on = [[copy(3, 0, c, up), copy(3, 6, c, down), copy(5, 2, c, up), copy(5, 8, c, down)] for c in range(CHUNKS)]
    for c in range(CHUNKS):
        for one in first[c] + along[c]:
            one.start()

    x = x_ref[...]
    cells = x.shape[0] // 3
    relative = x - jnp.sum(x, axis=1, keepdims=True) * (1.0 / V)
    once = lax.dot_general(relative, bend_ref[...], NT, precision=lax.Precision.HIGHEST, preferred_element_type=f32)
    twice = lax.dot_general(once, bend_ref[...], NT, precision=lax.Precision.HIGHEST, preferred_element_type=f32)
    square = jnp.sum(relative * relative, axis=1, keepdims=True)
    spread = (square[:cells] + square[cells:2 * cells] + square[2 * cells:]) * (1.0 / V)
    stretch = AREA_MODULUS * (spread / cell_ref[:, 0:1] - 1.0)
    alive = cell_ref[:, 1:2]
    for d in range(3):
        rows = slice(d * cells, (d + 1) * cells)
        internal_ref[rows] = -(BENDING_MODULUS * twice[rows] + stretch * relative[rows]) * alive

    for c in range(CHUNKS):
        for k in range(2):
            first[c][k].wait_recv()
            on[c][2 * k].start()
            on[c][2 * k + 1].start()
    keep.wait()
    for c in range(CHUNKS):
        for one in first[c]:
            one.wait_send()
        for one in along[c] + on[c]:
            one.wait()

def halo(own, x, bending, cell):
    size = own.shape[0]
    nx, ny = lax.axis_size("gx"), lax.axis_size("gy")
    vmem, anywhere = pl.BlockSpec(memory_space=pltpu.VMEM), pl.BlockSpec(memory_space=pl.ANY)
    return pl.pallas_call(
        functools.partial(halo_kernel, nx, ny),
        out_shape=(jax.ShapeDtypeStruct((9 * size, TILE), f32), jax.ShapeDtypeStruct(x.shape, f32)),
        in_specs=[anywhere, vmem, vmem, vmem],
        out_specs=(anywhere, vmem),
        scratch_shapes=[pltpu.SemaphoreType.DMA((9, CHUNKS)), pltpu.SemaphoreType.DMA((9, CHUNKS)), pltpu.SemaphoreType.DMA],
        compiler_params=pltpu.CompilerParams(collective_id=0, has_side_effects=True, vmem_limit_bytes=30 * 2**20),
        name="halo",
    )(own, x, bending, cell)

def moved(array, by_x, by_y):
    nx, ny = lax.axis_size("gx"), lax.axis_size("gy")
    pairs = [(i * ny + j, (i + by_x) % nx * ny + (j + by_y) % ny) for i in range(nx) for j in range(ny)]
    return lax.ppermute(array, ("gx", "gy"), pairs)

def on_device(solvent_pos, solvent_vel, pair_index, random_pairs, membrane_pos, membrane_vel, mem_vertex, mem_partner,
              bending, rest_size, cell_count):
    cells = rest_size.shape[0]
    vel = solvent_vel.reshape(3, BOXES, TILE)
    own = jnp.concatenate([solvent_pos.reshape(3, BOXES, TILE), vel], axis=0).reshape(6 * BOXES, TILE)
    alive = (jnp.arange(cells, dtype=jnp.int32) < cell_count[0]).astype(f32)
    tab, internal = halo(own, membrane_pos.reshape(3 * cells, V), bending, jnp.stack([rest_size, alive], axis=1))
    con, rea = contact(tab, membrane_pos, membrane_vel, mem_vertex, mem_partner, cell_count)
    back = [rea[3 * p + q] if (p, q) == (1, 1) else moved(rea[3 * p + q], p - 1, q - 1) for p in range(3) for q in range(3)]
    force = solvent(tab, pair_index, random_pairs)
    returned = sum(back[1:], back[0])
    push = jnp.array([SOLVENT_PUSH, 0.0, 0.0], f32)[:, None, None]
    solvent_velocity = (vel + TIME_STEP * (force + returned + push)).reshape(3, BOXES * TILE)
    touch = con.reshape(3, MB * TILE)[:, :membrane_pos.shape[1]]
    membrane_velocity = membrane_vel + TIME_STEP * (internal.reshape(membrane_pos.shape) + touch)
    return solvent_velocity, membrane_velocity

def solution(mesh):
    both = ("gx", "gy")
    flat, tiles = P(None, both), P(both, None)
    return jax.shard_map(
        on_device,
        mesh=mesh,
        in_specs=(flat, flat, tiles, P(both, None, None), flat, flat, tiles, tiles, P(), P(both), P(both)),
        out_specs=(flat, flat),
        check_vma=False,
    )
```

```python
import functools
from jax.sharding import PartitionSpec as P
import jax, jax.numpy as jnp
from jax import lax
from jax.experimental import pallas as pl
from jax.experimental.pallas import tpu as pltpu

f32, bf16 = jnp.float32, jnp.bfloat16
BOXES, TILE, PAIRS = 96, 128, 4
GROUP = 8
TIME_STEP = 0.01
SOLVENT_PUSH = 0.5
MESH = pl.DeviceIdType.MESH

def split3(v):
    p1 = v.astype(bf16).astype(f32)
    rest = v - p1
    p2 = rest.astype(bf16).astype(f32)
    return p1, p2, rest - p2

NT = (((1,), (1,)), ((), ()))

def part_of(blk):
    return (blk * 683) >> 16

def row_of(blk):
    return blk + part_of(blk) * (5 * BOXES)

def gather_block(tab_ref, blk, low, high, held, row):
    n = part_of(blk)
    p = (n * 11) >> 5
    dx = (p - 1).astype(f32) * 4.0
    dy = (n - 3 * p - 1).astype(f32) * 4.0
    block = tab_ref[pl.ds(blk + n * (5 * BOXES), 6, stride=BOXES), :]
    got = jnp.take_along_axis(block, low, axis=1, mode="promise_in_bounds")
    got = got + jnp.where(row == 0, dx, jnp.where(row == 1, dy, 0.0))
    return jnp.where(high == blk, got, held)

def box_centre(box, row8):
    cx = (box & 1).astype(f32) * 2.0 + 1.0
    cy = ((box >> 1) & 1).astype(f32) * 2.0 + 1.0
    cz = (box >> 2).astype(f32) * 2.0 + 1.0
    return jnp.where(row8 == 0, cx, jnp.where(row8 == 1, cy, jnp.where(row8 == 2, cz, 0.0)))

def own_features(own, row8):
    a, u = own[0:3], own[3:6] * 4.5
    aa = jnp.sum(a * a, axis=0, keepdims=True)
    au = jnp.sum(a * u, axis=0, keepdims=True)
    zero = jnp.zeros((3, TILE), f32)
    one = jnp.ones((1, TILE), f32)
    def left(q, const):
        q1, q2, q3 = split3(q)
        c1, c2, c3 = split3(const)
        last = jnp.where(row8 == 0, c1, jnp.where(row8 == 1, c2, jnp.where(row8 == 2, c3, 0.0)))
        return jnp.concatenate([q1, q1, q1, q2, q2, q3, last, jnp.zeros_like(last)], axis=0)
    ql = left(jnp.concatenate([-2.0 * a, zero, one, 0.0 * one], axis=0), aa)
    qs = left(jnp.concatenate([-u, -4.5 * a, 0.0 * one, 4.5 * one], axis=0), au)
    return jnp.concatenate([ql.T, qs.T], axis=0).astype(bf16)

def right_features(held, centre, row8):
    held = jnp.concatenate([held, held[0:2]], axis=0) - centre
    b, w = held[0:3], held[3:6]
    bb = jnp.sum(b * b, axis=0, keepdims=True)
    bw = jnp.sum(b * w, axis=0, keepdims=True)
    full = jnp.where(row8 == 6, bb, jnp.where(row8 == 7, bw, held))
    p1, p2, p3 = split3(full)
    ones = jnp.ones_like(p1)
    v1 = jnp.where(row8 == 3, 1.0, p1)
    return (jnp.concatenate([p1, p2, p3, p1, p2, p1, ones, ones], axis=0).astype(bf16),
            jnp.concatenate([v1, p2, p3, p3], axis=0).astype(bf16))

def pair_force(out, theta_ref, k, h):
    r2, s = out[:TILE], out[TILE:]
    th = jnp.concatenate([theta_ref[k * PAIRS + 2 * h], theta_ref[k * PAIRS + 2 * h + 1]], axis=1).astype(f32)
    r2 = jnp.maximum(r2, 1e-12)
    q = lax.rsqrt(r2)
    g = jnp.maximum(jnp.minimum(q, 10.0) * (1.0 - r2 * q), 0.0)
    force = g * (25.0 + 30.0 * th - g * s)
    fh = force.astype(bf16)
    return fh, (force - fh.astype(f32)).astype(bf16)

def pair_kernel(nx, ny, held_ref, theta_ref, own_ref, rea_ref, out_ref, back_ref, send_sem, recv_sem, own_sem):
    step = pl.program_id(0)
    row8 = lax.broadcasted_iota(jnp.int32, (8, TILE), 0)
    gx, gy = lax.axis_index("gx"), lax.axis_index("gy")
    size = 3 * BOXES

    def slot(ref, n):
        return ref.at[pl.ds(n * size, size)]

    def device(n):
        return (lax.rem(gx + n // 3 - 1 + nx, nx), lax.rem(gy + n % 3 - 1 + ny, ny))

    others = [n for n in range(9) if n != 4]
    sends = [pltpu.make_async_remote_copy(
        src_ref=slot(rea_ref, n), dst_ref=slot(back_ref, n), send_sem=send_sem.at[n], recv_sem=recv_sem.at[n],
        device_id=device(n), device_id_type=MESH) for n in others]
    keep = pltpu.make_async_copy(slot(rea_ref, 4), slot(back_ref, 4), own_sem)

    @pl.when(step == 0)
    def _():
        barrier = pltpu.get_barrier_semaphore()
        for n in others:
            pl.semaphore_signal(barrier, inc=1, device_id=device(n), device_id_type=MESH)
        pl.semaphore_wait(barrier, 8)
        keep.start()
        for send in sends:
            send.start()

    @pl.loop(0, GROUP, unroll=GROUP)
    def _(k):
        box = step * GROUP + k
        centre = box_centre(box, row8)
        own = own_ref[pl.ds(box, 6, stride=BOXES), :] - centre[0:6]
        lhs = own_features(own, row8)
        acc = jnp.zeros((32, TILE), f32)
        for h in range(2):
            feats = [right_features(held_ref[k * PAIRS + 2 * h + j, 0:6, :], centre, row8) for j in range(2)]
            rhs, sums = [jnp.concatenate(parts, axis=1) for parts in zip(*feats)]
            out = jnp.dot(lhs, rhs, preferred_element_type=f32)
            for force in pair_force(out, theta_ref, k, h):
                acc += lax.dot_general(sums, force, NT, preferred_element_type=f32)
        out_ref[pl.ds(box, 3, stride=BOXES), :] = own[0:3] * acc[3:4] - (acc[0:8] + acc[8:16] + acc[16:24])[0:3]

    @pl.when(step == BOXES // GROUP - 1)
    def _():
        keep.wait()
        for send in sends:
            send.wait()
        total = out_ref[...]
        for n in range(9):
            total += back_ref[pl.ds(n * size, size), :]
        row = lax.broadcasted_iota(jnp.int32, (size, TILE), 0)
        total += jnp.where(row < BOXES, SOLVENT_PUSH, 0.0)
        out_ref[...] = own_ref[pl.ds(size, size), :] + TIME_STEP * total

def pairs(held, theta, own, rea):
    nx, ny = lax.axis_size("gx"), lax.axis_size("gy")
    size = 3 * BOXES
    return pl.pallas_call(
        functools.partial(pair_kernel, nx, ny),
        out_shape=jax.ShapeDtypeStruct((size, TILE), f32),
        grid=(BOXES // GROUP,),
        in_specs=[
            pl.BlockSpec((GROUP * PAIRS, 8, TILE), lambda i: (i, 0, 0)),
            pl.BlockSpec((GROUP * PAIRS, TILE, TILE), lambda i: (i, 0, 0)),
            pl.BlockSpec((2 * size, TILE), lambda i: (0, 0)),
            pl.BlockSpec(memory_space=pl.ANY),
        ],
        out_specs=pl.BlockSpec((size, TILE), lambda i: (0, 0)),
        scratch_shapes=[pltpu.VMEM((9 * size, TILE), f32), pltpu.SemaphoreType.DMA((9,)), pltpu.SemaphoreType.DMA((9,)), pltpu.SemaphoreType.DMA],
        compiler_params=pltpu.CompilerParams(collective_id=1, has_side_effects=True, vmem_limit_bytes=40 * 2**20),
        name="pairs",
    )(held, theta, own, rea)

def block_range(index, unused):
    high = index >> 7
    full = index >= unused
    first = jnp.min(jnp.where(full, (unused >> 7) - 1, high), axis=1)
    last = jnp.max(jnp.where(full, 0, high), axis=1)
    return first, jnp.maximum(first, last)


V = 642
MEM_TILES = 64
MB = 96
WIN = 8
SPAN = 16
UNG, UNC, UNS = 16, 8, 16

def gather_window(tab_ref, base, low, high, held):
    for k in range(WIN):
        block = tab_ref[pl.ds(base + k, 6, stride=MB), :]
        got = jnp.take_along_axis(block, low, axis=1, mode="promise_in_bounds")
        held = jnp.where(high == base + k, got, held)
    return held

def vertex_sums(base, low, high, pieces, rowt, row16):
    onehot = (rowt == low).astype(f32).astype(bf16)
    hit = high == row16 + base
    left = jnp.concatenate([jnp.where(hit, p[c:c + 1], 0.0) for p in pieces for c in range(3)], axis=0).astype(bf16)
    out = lax.dot_general(left, onehot, NT, preferred_element_type=f32)
    return out[:3 * SPAN] + out[3 * SPAN:]

def add_vertex(con_ref, base, out):
    for c in range(3):
        con_ref[c, pl.ds(base, SPAN), :] += out[c * SPAN:(c + 1) * SPAN]

def partner_sums(blk, low, high, pieces, rowt):
    onehot = ((rowt == low) & (high == blk)).astype(f32).astype(bf16)
    out = lax.dot_general(pieces, onehot, NT, preferred_element_type=f32)
    return (out[0:8] + out[8:16])[0:3]

def add_partner(rea_ref, blk, out):
    rea_ref[pl.ds(blk + part_of(blk) * (2 * BOXES), 3, stride=BOXES), :] += out

def contact_kernel(plo, phi, vlo, vhi, slo, shi, count, par_ref, ver_ref, idx_ref, tab_ref, mem_ref, con_ref, rea_ref, held_ref, lh_ref, rh_ref, fo_ref):
    row6 = lax.broadcasted_iota(jnp.int32, (6, TILE), 0)
    row8 = lax.broadcasted_iota(jnp.int32, (8, TILE), 0)
    rowt = lax.broadcasted_iota(jnp.int32, (TILE, TILE), 0)
    row16 = lax.broadcasted_iota(jnp.int32, (SPAN, TILE), 0)
    far = jnp.where(row6 < 3, 1000.0, 0.0)
    alive_end = count[0] * V
    con_ref[...] = jnp.zeros_like(con_ref)
    rea_ref[...] = jnp.zeros_like(rea_ref)

    @pl.loop(0, idx_ref.shape[0] // UNG)
    def _(part):
        spread = jnp.int32(0)
        for k in range(UNG):
            t = part * UNG + k
            first = slo[t]
            spread = jnp.maximum(spread, shi[t] - first)
            index = jnp.broadcast_to(idx_ref[pl.ds(t, 1), :], (6, TILE))
            held_ref[t, 0:6, :] = gather_block(tab_ref, first, index & 127, index >> 7, far, row6)

        @pl.when(spread > 0)
        def _():
            @pl.loop(0, UNG)
            def _(k):
                t = part * UNG + k
                index = jnp.broadcast_to(idx_ref[pl.ds(t, 1), :], (6, TILE))

                @pl.loop(slo[t] + 1, shi[t] + 1)
                def _(blk):
                    held_ref[t, 0:6, :] = gather_block(tab_ref, blk, index & 127, index >> 7, held_ref[t, 0:6, :], row6)

    @pl.loop(0, MEM_TILES // UNG)
    def _(part):
        spread = jnp.int32(0)
        vspread = jnp.int32(0)
        for k in range(UNG):
            t = part * UNG + k
            first = plo[t]
            spread = jnp.maximum(spread, phi[t] - first)
            vspread = jnp.maximum(vspread, vhi[t] - vlo[t])
            index = jnp.broadcast_to(par_ref[pl.ds(t, 1), :], (6, TILE))
            rh_ref[t, 0:6, :] = gather_block(tab_ref, first, index & 127, index >> 7, far, row6)
            vert = jnp.broadcast_to(ver_ref[pl.ds(t, 1), :], (6, TILE))
            high = jnp.where(vert < alive_end, vert >> 7, -1)
            lh_ref[t, 0:6, :] = gather_window(mem_ref, vlo[t], vert & 127, high, far)

        @pl.when(spread > 0)
        def _():
            @pl.loop(0, UNG)
            def _(k):
                t = part * UNG + k
                index = jnp.broadcast_to(par_ref[pl.ds(t, 1), :], (6, TILE))

                @pl.loop(plo[t] + 1, phi[t] + 1)
                def _(blk):
                    rh_ref[t, 0:6, :] = gather_block(tab_ref, blk, index & 127, index >> 7, rh_ref[t, 0:6, :], row6)

        @pl.when(vspread >= WIN)
        def _():
            @pl.loop(0, UNG)
            def _(k):
                t = part * UNG + k
                vert = jnp.broadcast_to(ver_ref[pl.ds(t, 1), :], (6, TILE))
                high = jnp.where(vert < alive_end, vert >> 7, -1)

                @pl.loop(1, (vhi[t] - vlo[t]) // WIN + 1)
                def _(j):
                    lh_ref[t, 0:6, :] = gather_window(mem_ref, vlo[t] + j * WIN, vert & 127, high, lh_ref[t, 0:6, :])

    def centre_of(blk):
        n = part_of(blk)
        box = blk - BOXES * n
        p = (n * 11) >> 5
        cx = ((p - 1) * 4 + (box & 1) * 2 + 1).astype(f32)
        cy = ((n - 3 * p - 1) * 4 + ((box >> 1) & 1) * 2 + 1).astype(f32)
        cz = ((box >> 2) * 2 + 1).astype(f32)
        return jnp.where(row8 == 0, cx, jnp.where(row8 == 1, cy, jnp.where(row8 == 2, cz, 0.0)))

    def store_forces(t, r2, s, centre, wa, wb):
        r2 = jnp.maximum(r2, 1e-12)
        q = lax.rsqrt(r2)
        g = jnp.maximum(jnp.minimum(q, 10.0) * (1.0 - r2 * q), 0.0)
        force = g * (25.0 - g * s)
        fh = force.astype(bf16)
        fl = (force - fh.astype(f32)).astype(bf16)
        con = lax.dot_general(wb, fh, NT, preferred_element_type=f32) + lax.dot_general(wb, fl, NT, preferred_element_type=f32)
        rea = jnp.dot(wa, fh, preferred_element_type=f32) + jnp.dot(wa, fl, preferred_element_type=f32)
        fo_ref[t, 0:8, :] = (lh_ref[t] - centre) * con[3:4] - (con[0:8] + con[8:16] + con[16:24])
        fo_ref[t, 8:16, :] = (rh_ref[t] - centre) * rea[3:4] - (rea[0:8] + rea[8:16] + rea[16:24])

    unit = [jnp.where(row8 == c, 1.0, 0.0) for c in range(6)]
    scale = jnp.where(row8 < 3, 1.0, 4.5)

    @pl.loop(0, MEM_TILES // UNC)
    def _(part):
        spread = jnp.int32(0)
        for k in range(UNC):
            t = part * UNC + k
            spread = jnp.maximum(spread, phi[t] - plo[t])
            centre = centre_of(plo[t])
            left, right = lh_ref[t, 0:6, :], rh_ref[t, 0:6, :]
            lhs = own_features(left - centre[0:6], row8)
            rhs, wb = right_features(right, centre, row8)
            wa = right_features(left, centre, row8)[1]
            out = jnp.dot(lhs, rhs, preferred_element_type=f32)
            store_forces(t, out[:TILE], out[TILE:], centre, wa, wb)

        @pl.when(spread > 0)
        def _():
            @pl.loop(0, UNC)
            def _(k):
                t = part * UNC + k
                centre = centre_of(plo[t])
                left, right = lh_ref[t, 0:6, :], rh_ref[t, 0:6, :]
                wb, wa = right_features(right, centre, row8)[1], right_features(left, centre, row8)[1]
                live6 = row8 < 6
                a1, a2, a3 = split3(jnp.where(live6, lh_ref[t] - centre, 0.0) * scale)
                b1, b2, b3 = split3(jnp.where(live6, rh_ref[t] - centre, 0.0) * scale)
                one = jnp.ones_like(a1)
                left = jnp.concatenate([a1, a2, a3, one, one, one], axis=0).T.astype(bf16)
                diffs = []
                for c in range(6):
                    rhs = jnp.concatenate([unit[c], unit[c], unit[c], -b1 * unit[c], -b2 * unit[c], -b3 * unit[c]], axis=0).astype(bf16)
                    diffs.append(jnp.dot(left, rhs, preferred_element_type=f32))
                dx, dy, dz, du, dv, dw = diffs
                store_forces(t, dx * dx + dy * dy + dz * dz, dx * du + dy * dv + dz * dw, centre, wa, wb)

    def pieces_of(t):
        con, rea = fo_ref[t, 0:8, :], jnp.where(row8 < 3, fo_ref[t, 8:16, :], 0.0)
        c1 = con.astype(bf16).astype(f32)
        r1 = rea.astype(bf16).astype(f32)
        return (c1, con - c1), jnp.concatenate([r1, rea - r1], axis=0).astype(bf16)

    @pl.loop(0, MEM_TILES // UNS)
    def _(part):
        more = jnp.int32(0)
        sums = []
        for k in range(UNS):
            t = part * UNS + k
            con, rea = pieces_of(t)
            vert, index = ver_ref[pl.ds(t, 1), :], par_ref[pl.ds(t, 1), :]
            base = pl.multiple_of((vlo[t] >> 3) << 3, 8)
            more = jnp.maximum(more, jnp.maximum(phi[t] - plo[t], (vhi[t] - base) >> 4))
            sums.append((base, vertex_sums(base, vert & 127, vert >> 7, con, rowt, row16),
                         plo[t], partner_sums(plo[t], index & 127, index >> 7, rea, rowt)))
        for base, con, blk, rea in sums:
            add_vertex(con_ref, base, con)
            add_partner(rea_ref, blk, rea)

        @pl.when(more > 0)
        def _():
            @pl.loop(0, UNS)
            def _(k):
                t = part * UNS + k
                con, rea = pieces_of(t)
                vert, index = ver_ref[pl.ds(t, 1), :], par_ref[pl.ds(t, 1), :]
                base = (vlo[t] >> 3) << 3

                @pl.loop(1, ((vhi[t] - base) >> 4) + 1)
                def _(j):
                    at = pl.multiple_of(base + j * SPAN, 8)
                    add_vertex(con_ref, at, vertex_sums(at, vert & 127, vert >> 7, con, rowt, row16))

                @pl.loop(plo[t] + 1, phi[t] + 1)
                def _(blk):
                    add_partner(rea_ref, blk, partner_sums(blk, index & 127, index >> 7, rea, rowt))

def contact(tab, mem, vertex, partner, index, count):
    smem, vmem = pl.BlockSpec(memory_space=pltpu.SMEM), pl.BlockSpec(memory_space=pltpu.VMEM)
    unused = 9 * BOXES * TILE
    tile = pltpu.VMEM((MEM_TILES, 8, TILE), f32)
    return pl.pallas_call(
        contact_kernel,
        out_shape=(
            jax.ShapeDtypeStruct((3, MB, TILE), f32),
            jax.ShapeDtypeStruct((9 * 3 * BOXES, TILE), f32),
            jax.ShapeDtypeStruct((index.shape[0], 8, TILE), f32),
        ),
        in_specs=[smem] * 7 + [vmem] * 5,
        out_specs=(vmem, vmem, vmem),
        scratch_shapes=[tile, tile, pltpu.VMEM((MEM_TILES, 16, TILE), f32)],
        compiler_params=pltpu.CompilerParams(vmem_limit_bytes=40 * 2**20),
        name="contact",
    )(*block_range(partner, unused), *block_range(vertex, MB * TILE), *block_range(index, unused), count,
      partner, vertex, index, tab, mem)

BENDING_MODULUS = 20.0
AREA_MODULUS = 40.0

CHUNKS = 3

def halo_kernel(nx, ny, own_ref, x_ref, bend_ref, cell_ref, tab_ref, internal_ref, send_sem, recv_sem, own_sem):
    gx, gy = lax.axis_index("gx"), lax.axis_index("gy")
    up, down = (lax.rem(gx + 1, nx), gy), (lax.rem(gx + nx - 1, nx), gy)
    right, left = (gx, lax.rem(gy + 1, ny)), (gx, lax.rem(gy + ny - 1, ny))
    size = own_ref.shape[0]
    part = size // CHUNKS

    barrier = pltpu.get_barrier_semaphore()
    for device in (up, down, right, left):
        pl.semaphore_signal(barrier, inc=1, device_id=device, device_id_type=MESH)
    pl.semaphore_wait(barrier, 4)

    def slot(n, c):
        return tab_ref.at[pl.ds(n * size + c * part, part)]

    def copy(source, n, c, device):
        src = own_ref.at[pl.ds(c * part, part)] if source is None else slot(source, c)
        return pltpu.make_async_remote_copy(
            src_ref=src, dst_ref=slot(n, c), send_sem=send_sem.at[n, c], recv_sem=recv_sem.at[n, c],
            device_id=device, device_id_type=MESH)

    keep = pltpu.make_async_copy(own_ref, tab_ref.at[pl.ds(4 * size, size)], own_sem)
    keep.start()
    first = [[copy(None, 3, c, right), copy(None, 5, c, left)] for c in range(CHUNKS)]
    along = [[copy(None, 1, c, up), copy(None, 7, c, down)] for c in range(CHUNKS)]
    on = [[copy(3, 0, c, up), copy(3, 6, c, down), copy(5, 2, c, up), copy(5, 8, c, down)] for c in range(CHUNKS)]
    for c in range(CHUNKS):
        for one in first[c] + along[c]:
            one.start()

    x = x_ref[...]
    cells = x.shape[0] // 3
    relative = x - jnp.sum(x, axis=1, keepdims=True) * (1.0 / V)
    once = lax.dot_general(relative, bend_ref[...], NT, precision=lax.Precision.HIGHEST, preferred_element_type=f32)
    twice = lax.dot_general(once, bend_ref[...], NT, precision=lax.Precision.HIGHEST, preferred_element_type=f32)
    square = jnp.sum(relative * relative, axis=1, keepdims=True)
    spread = (square[:cells] + square[cells:2 * cells] + square[2 * cells:]) * (1.0 / V)
    stretch = AREA_MODULUS * (spread / cell_ref[:, 0:1] - 1.0)
    alive = cell_ref[:, 1:2]
    for d in range(3):
        rows = slice(d * cells, (d + 1) * cells)
        internal_ref[rows] = -(BENDING_MODULUS * twice[rows] + stretch * relative[rows]) * alive

    for c in range(CHUNKS):
        for k in range(2):
            first[c][k].wait_recv()
            on[c][2 * k].start()
            on[c][2 * k + 1].start()
    keep.wait()
    for c in range(CHUNKS):
        for one in first[c]:
            one.wait_send()
        for one in along[c] + on[c]:
            one.wait()

def halo(own, x, bending, cell):
    size = own.shape[0]
    nx, ny = lax.axis_size("gx"), lax.axis_size("gy")
    vmem, anywhere = pl.BlockSpec(memory_space=pltpu.VMEM), pl.BlockSpec(memory_space=pl.ANY)
    return pl.pallas_call(
        functools.partial(halo_kernel, nx, ny),
        out_shape=(jax.ShapeDtypeStruct((9 * size, TILE), f32), jax.ShapeDtypeStruct(x.shape, f32)),
        in_specs=[anywhere, vmem, vmem, vmem],
        out_specs=(anywhere, vmem),
        scratch_shapes=[pltpu.SemaphoreType.DMA((9, CHUNKS)), pltpu.SemaphoreType.DMA((9, CHUNKS)), pltpu.SemaphoreType.DMA],
        compiler_params=pltpu.CompilerParams(collective_id=0, has_side_effects=True, vmem_limit_bytes=30 * 2**20),
        name="halo",
    )(own, x, bending, cell)

def on_device(solvent_pos, solvent_vel, pair_index, random_pairs, membrane_pos, membrane_vel, mem_vertex, mem_partner,
              bending, rest_size, cell_count):
    cells = rest_size.shape[0]
    own = jnp.concatenate([solvent_pos, solvent_vel], axis=0).reshape(6 * BOXES, TILE)
    alive = (jnp.arange(cells, dtype=jnp.int32) < cell_count[0]).astype(f32)
    tab, internal = halo(own, membrane_pos.reshape(3 * cells, V), bending, jnp.stack([rest_size, alive], axis=1))
    mem = jnp.concatenate([membrane_pos, membrane_vel], axis=0)
    mem = jnp.pad(mem, ((0, 0), (0, MB * TILE - mem.shape[1]))).reshape(6 * MB, TILE)
    con, rea, held = contact(tab, mem, mem_vertex, mem_partner, pair_index, cell_count)
    solvent_velocity = pairs(held, random_pairs, own, rea).reshape(3, BOXES * TILE)
    touch = con.reshape(3, MB * TILE)[:, :membrane_pos.shape[1]]
    membrane_velocity = membrane_vel + TIME_STEP * (internal.reshape(membrane_pos.shape) + touch)
    return solvent_velocity, membrane_velocity

def solution(mesh):
    both = ("gx", "gy")
    flat, tiles = P(None, both), P(both, None)
    return jax.shard_map(
        on_device,
        mesh=mesh,
        in_specs=(flat, flat, tiles, P(both, None, None), flat, flat, tiles, tiles, P(), P(both), P(both)),
        out_specs=(flat, flat),
        check_vma=False,
    )
```

```python
import functools
from jax.sharding import PartitionSpec as P
import jax, jax.numpy as jnp
from jax import lax
from jax.experimental import pallas as pl
from jax.experimental.pallas import tpu as pltpu

f32, bf16 = jnp.float32, jnp.bfloat16
BOXES, TILE, PAIRS = 96, 128, 4
GROUP = 8
TIME_STEP = 0.01
SOLVENT_PUSH = 0.5
MESH = pl.DeviceIdType.MESH

def split3(v):
    p1 = v.astype(bf16).astype(f32)
    rest = v - p1
    p2 = rest.astype(bf16).astype(f32)
    return p1, p2, rest - p2

NT = (((1,), (1,)), ((), ()))

def part_of(blk):
    return (blk * 683) >> 16

def row_of(blk):
    return blk + part_of(blk) * (5 * BOXES)

def gather_block(tab_ref, blk, low, high, held, row):
    n = part_of(blk)
    p = (n * 11) >> 5
    dx = (p - 1).astype(f32) * 4.0
    dy = (n - 3 * p - 1).astype(f32) * 4.0
    block = tab_ref[pl.ds(blk + n * (5 * BOXES), 6, stride=BOXES), :]
    got = jnp.take_along_axis(block, low, axis=1, mode="promise_in_bounds")
    got = got + jnp.where(row == 0, dx, jnp.where(row == 1, dy, 0.0))
    return jnp.where(high == blk, got, held)

def box_centre(box, row8):
    cx = (box & 1).astype(f32) * 2.0 + 1.0
    cy = ((box >> 1) & 1).astype(f32) * 2.0 + 1.0
    cz = (box >> 2).astype(f32) * 2.0 + 1.0
    return jnp.where(row8 == 0, cx, jnp.where(row8 == 1, cy, jnp.where(row8 == 2, cz, 0.0)))

def own_features(own, row8):
    a, u = own[0:3], own[3:6] * 4.5
    aa = jnp.sum(a * a, axis=0, keepdims=True)
    au = jnp.sum(a * u, axis=0, keepdims=True)
    zero = jnp.zeros((3, TILE), f32)
    one = jnp.ones((1, TILE), f32)
    def left(q, const):
        q1, q2, q3 = split3(q)
        c1, c2, c3 = split3(const)
        last = jnp.where(row8 == 0, c1, jnp.where(row8 == 1, c2, jnp.where(row8 == 2, c3, 0.0)))
        return jnp.concatenate([q1, q1, q1, q2, q2, q3, last, jnp.zeros_like(last)], axis=0)
    ql = left(jnp.concatenate([-2.0 * a, zero, one, 0.0 * one], axis=0), aa)
    qs = left(jnp.concatenate([-u, -4.5 * a, 0.0 * one, 4.5 * one], axis=0), au)
    return jnp.concatenate([ql.T, qs.T], axis=0).astype(bf16)

def right_features(held, centre, row8):
    held = jnp.concatenate([held, held[0:2]], axis=0) - centre
    b, w = held[0:3], held[3:6]
    bb = jnp.sum(b * b, axis=0, keepdims=True)
    bw = jnp.sum(b * w, axis=0, keepdims=True)
    full = jnp.where(row8 == 6, bb, jnp.where(row8 == 7, bw, held))
    p1, p2, p3 = split3(full)
    ones = jnp.ones_like(p1)
    v1 = jnp.where(row8 == 3, 1.0, p1)
    return (jnp.concatenate([p1, p2, p3, p1, p2, p1, ones, ones], axis=0).astype(bf16),
            jnp.concatenate([v1, p2, p3, p3], axis=0).astype(bf16))

def pair_force(out, theta_ref, k, h):
    r2, s = out[:TILE], out[TILE:]
    th = jnp.concatenate([theta_ref[k * PAIRS + 2 * h], theta_ref[k * PAIRS + 2 * h + 1]], axis=1).astype(f32)
    r2 = jnp.maximum(r2, 1e-12)
    q = lax.rsqrt(r2)
    g = jnp.maximum(jnp.minimum(q, 10.0) * (1.0 - r2 * q), 0.0)
    force = g * (25.0 + 30.0 * th - g * s)
    fh = force.astype(bf16)
    return fh, (force - fh.astype(f32)).astype(bf16)

def pair_kernel(nx, ny, held_ref, theta_ref, own_ref, rea_ref, out_ref, row_ref, far_ref, back_ref, send_sem, recv_sem, own_sem):
    step = pl.program_id(0)
    row8 = lax.broadcasted_iota(jnp.int32, (8, TILE), 0)
    gx, gy = lax.axis_index("gx"), lax.axis_index("gy")
    size = 3 * BOXES
    down, up = (lax.rem(gx + nx - 1, nx), gy), (lax.rem(gx + 1, nx), gy)
    left, right = (gx, lax.rem(gy + ny - 1, ny)), (gx, lax.rem(gy + 1, ny))

    def send(src, dst, k, device):
        return pltpu.make_async_remote_copy(
            src_ref=src, dst_ref=dst, send_sem=send_sem.at[k], recv_sem=recv_sem.at[k], device_id=device, device_id_type=MESH)

    keep = pltpu.make_async_copy(rea_ref.at[pl.ds(3 * size, 3 * size)], row_ref, own_sem)
    rows = [send(rea_ref.at[pl.ds(0, 3 * size)], far_ref.at[0], 0, down),
            send(rea_ref.at[pl.ds(6 * size, 3 * size)], far_ref.at[1], 1, up)]
    columns = [send(row_ref.at[pl.ds(0, size)], back_ref.at[0], 2, left),
               send(row_ref.at[pl.ds(2 * size, size)], back_ref.at[1], 3, right)]

    @pl.when(step == 0)
    def _():
        barrier = pltpu.get_barrier_semaphore()
        for device in (down, up, left, right):
            pl.semaphore_signal(barrier, inc=1, device_id=device, device_id_type=MESH)
        pl.semaphore_wait(barrier, 4)
        keep.start()
        for one in rows:
            one.start()

    @pl.when(step == BOXES // GROUP // 2)
    def _():
        keep.wait()
        for one in rows:
            one.wait()
        row_ref[...] += far_ref[0] + far_ref[1]
        for one in columns:
            one.start()

    @pl.loop(0, GROUP, unroll=GROUP)
    def _(k):
        box = step * GROUP + k
        centre = box_centre(box, row8)
        own = own_ref[pl.ds(box, 6, stride=BOXES), :] - centre[0:6]
        lhs = own_features(own, row8)
        acc = jnp.zeros((32, TILE), f32)
        for h in range(2):
            feats = [right_features(held_ref[k * PAIRS + 2 * h + j, 0:6, :], centre, row8) for j in range(2)]
            rhs, sums = [jnp.concatenate(parts, axis=1) for parts in zip(*feats)]
            out = jnp.dot(lhs, rhs, preferred_element_type=f32)
            for force in pair_force(out, theta_ref, k, h):
                acc += lax.dot_general(sums, force, NT, preferred_element_type=f32)
        out_ref[pl.ds(box, 3, stride=BOXES), :] = own[0:3] * acc[3:4] - (acc[0:8] + acc[8:16] + acc[16:24])[0:3]

    @pl.when(step == BOXES // GROUP - 1)
    def _():
        for one in columns:
            one.wait()
        total = out_ref[...] + row_ref[pl.ds(size, size), :] + back_ref[0] + back_ref[1]
        row = lax.broadcasted_iota(jnp.int32, (size, TILE), 0)
        total += jnp.where(row < BOXES, SOLVENT_PUSH, 0.0)
        out_ref[...] = own_ref[pl.ds(size, size), :] + TIME_STEP * total

def pairs(held, theta, tab, rea):
    nx, ny = lax.axis_size("gx"), lax.axis_size("gy")
    size = 3 * BOXES
    return pl.pallas_call(
        functools.partial(pair_kernel, nx, ny),
        out_shape=jax.ShapeDtypeStruct((size, TILE), f32),
        grid=(BOXES // GROUP,),
        in_specs=[
            pl.BlockSpec((GROUP * PAIRS, 8, TILE), lambda i: (i, 0, 0)),
            pl.BlockSpec((GROUP * PAIRS, TILE, TILE), lambda i: (i, 0, 0)),
            pl.BlockSpec((2 * size, TILE), lambda i: (4, 0)),
            pl.BlockSpec(memory_space=pl.ANY),
        ],
        out_specs=pl.BlockSpec((size, TILE), lambda i: (0, 0)),
        scratch_shapes=[pltpu.VMEM((3 * size, TILE), f32), pltpu.VMEM((2, 3 * size, TILE), f32), pltpu.VMEM((2, size, TILE), f32),
                        pltpu.SemaphoreType.DMA((4,)), pltpu.SemaphoreType.DMA((4,)), pltpu.SemaphoreType.DMA],
        compiler_params=pltpu.CompilerParams(collective_id=1, has_side_effects=True, vmem_limit_bytes=40 * 2**20),
        name="pairs",
    )(held, theta, tab, rea)


V = 642
MEM_TILES = 64
MB = 96
WIN = 8
SPAN = 16
UNG, UNC, UNS = 16, 8, 16
P_LOW, P_HIGH, V_LOW, V_HIGH = 6, 7, 8, 9

def gather_window(tab_ref, base, low, high, held):
    for k in range(WIN):
        block = tab_ref[pl.ds(base + k, 6, stride=MB), :]
        got = jnp.take_along_axis(block, low, axis=1, mode="promise_in_bounds")
        held = jnp.where(high == base + k, got, held)
    return held

def vertex_sums(base, low, high, pieces, rowt, row16):
    onehot = (rowt == low).astype(f32).astype(bf16)
    hit = high == row16 + base
    left = jnp.concatenate([jnp.where(hit, p[c:c + 1], 0.0) for p in pieces for c in range(3)], axis=0).astype(bf16)
    out = lax.dot_general(left, onehot, NT, preferred_element_type=f32)
    return out[:3 * SPAN] + out[3 * SPAN:]

def add_vertex(con_ref, base, out):
    for c in range(3):
        con_ref[c, pl.ds(base, SPAN), :] += out[c * SPAN:(c + 1) * SPAN]

def partner_sums(blk, low, high, pieces, rowt):
    onehot = ((rowt == low) & (high == blk)).astype(f32).astype(bf16)
    out = lax.dot_general(pieces, onehot, NT, preferred_element_type=f32)
    return (out[0:8] + out[8:16])[0:3]

def add_partner(rea_ref, blk, out):
    rea_ref[pl.ds(blk + part_of(blk) * (2 * BOXES), 3, stride=BOXES), :] += out

def contact_kernel(range_ref, count, par_ref, ver_ref, idx_ref, tab_ref, mem_ref, internal_ref, vel_ref, rea_ref, held_ref, out_ref, con_ref, lh_ref, rh_ref, fo_ref, force_ref, sum_ref):
    row6 = lax.broadcasted_iota(jnp.int32, (6, TILE), 0)
    row8 = lax.broadcasted_iota(jnp.int32, (8, TILE), 0)
    rowt = lax.broadcasted_iota(jnp.int32, (TILE, TILE), 0)
    row16 = lax.broadcasted_iota(jnp.int32, (SPAN, TILE), 0)
    far = jnp.where(row6 < 3, 1000.0, 0.0)
    alive_end = count[0] * V
    con_ref[...] = jnp.zeros_like(con_ref)
    rea_ref[...] = jnp.zeros_like(rea_ref)

    @pl.loop(0, idx_ref.shape[0] // UNG)
    def _(part):
        spread = jnp.int32(0)
        for k in range(UNG):
            t = part * UNG + k
            first = range_ref[t >> 7, t & 127]
            spread = jnp.maximum(spread, range_ref[(t >> 7) + 3, t & 127] - first)
            index = jnp.broadcast_to(idx_ref[pl.ds(t, 1), :], (6, TILE))
            held_ref[t, 0:6, :] = gather_block(tab_ref, first, index & 127, index >> 7, far, row6)

        @pl.when(spread > 0)
        def _():
            @pl.loop(0, UNG)
            def _(k):
                t = part * UNG + k
                index = jnp.broadcast_to(idx_ref[pl.ds(t, 1), :], (6, TILE))

                @pl.loop(range_ref[t >> 7, t & 127] + 1, range_ref[(t >> 7) + 3, t & 127] + 1)
                def _(blk):
                    held_ref[t, 0:6, :] = gather_block(tab_ref, blk, index & 127, index >> 7, held_ref[t, 0:6, :], row6)

    @pl.loop(0, MEM_TILES // UNG)
    def _(part):
        spread = jnp.int32(0)
        vspread = jnp.int32(0)
        for k in range(UNG):
            t = part * UNG + k
            first = range_ref[P_LOW, t]
            spread = jnp.maximum(spread, range_ref[P_HIGH, t] - first)
            vspread = jnp.maximum(vspread, range_ref[V_HIGH, t] - range_ref[V_LOW, t])
            index = jnp.broadcast_to(par_ref[pl.ds(t, 1), :], (6, TILE))
            rh_ref[t, 0:6, :] = gather_block(tab_ref, first, index & 127, index >> 7, far, row6)
            vert = jnp.broadcast_to(ver_ref[pl.ds(t, 1), :], (6, TILE))
            high = jnp.where(vert < alive_end, vert >> 7, -1)
            lh_ref[t, 0:6, :] = gather_window(mem_ref, range_ref[V_LOW, t], vert & 127, high, far)

        @pl.when(spread > 0)
        def _():
            @pl.loop(0, UNG)
            def _(k):
                t = part * UNG + k
                index = jnp.broadcast_to(par_ref[pl.ds(t, 1), :], (6, TILE))

                @pl.loop(range_ref[P_LOW, t] + 1, range_ref[P_HIGH, t] + 1)
                def _(blk):
                    rh_ref[t, 0:6, :] = gather_block(tab_ref, blk, index & 127, index >> 7, rh_ref[t, 0:6, :], row6)

        @pl.when(vspread >= WIN)
        def _():
            @pl.loop(0, UNG)
            def _(k):
                t = part * UNG + k
                vert = jnp.broadcast_to(ver_ref[pl.ds(t, 1), :], (6, TILE))
                high = jnp.where(vert < alive_end, vert >> 7, -1)

                @pl.loop(1, (range_ref[V_HIGH, t] - range_ref[V_LOW, t]) // WIN + 1)
                def _(j):
                    lh_ref[t, 0:6, :] = gather_window(mem_ref, range_ref[V_LOW, t] + j * WIN, vert & 127, high, lh_ref[t, 0:6, :])

    def centre_of(blk):
        n = part_of(blk)
        box = blk - BOXES * n
        p = (n * 11) >> 5
        cx = ((p - 1) * 4 + (box & 1) * 2 + 1).astype(f32)
        cy = ((n - 3 * p - 1) * 4 + ((box >> 1) & 1) * 2 + 1).astype(f32)
        cz = ((box >> 2) * 2 + 1).astype(f32)
        return jnp.where(row8 == 0, cx, jnp.where(row8 == 1, cy, jnp.where(row8 == 2, cz, 0.0)))

    def store_forces(t, r2, s, wa, wb):
        r2 = jnp.maximum(r2, 1e-12)
        q = lax.rsqrt(r2)
        g = jnp.maximum(jnp.minimum(q, 10.0) * (1.0 - r2 * q), 0.0)
        force = g * (25.0 - g * s)
        force_ref[0, t] = force.astype(bf16)
        force_ref[1, t] = (force - force_ref[0, t].astype(f32)).astype(bf16)
        sum_ref[0, t] = wa
        sum_ref[1, t] = wb

    unit = [jnp.where(row8 == c, 1.0, 0.0) for c in range(6)]
    scale = jnp.where(row8 < 3, 1.0, 4.5)

    @pl.loop(0, MEM_TILES // UNC)
    def _(part):
        spread = jnp.int32(0)
        for k in range(UNC):
            t = part * UNC + k
            spread = jnp.maximum(spread, range_ref[P_HIGH, t] - range_ref[P_LOW, t])
            centre = centre_of(range_ref[P_LOW, t])
            left, right = lh_ref[t, 0:6, :], rh_ref[t, 0:6, :]
            lhs = own_features(left - centre[0:6], row8)
            rhs, wb = right_features(right, centre, row8)
            wa = right_features(left, centre, row8)[1]
            out = jnp.dot(lhs, rhs, preferred_element_type=f32)
            store_forces(t, out[:TILE], out[TILE:], wa, wb)

        @pl.when(spread > 0)
        def _():
            @pl.loop(0, UNC)
            def _(k):
                t = part * UNC + k
                centre = centre_of(range_ref[P_LOW, t])
                left, right = lh_ref[t, 0:6, :], rh_ref[t, 0:6, :]
                wb, wa = right_features(right, centre, row8)[1], right_features(left, centre, row8)[1]
                live6 = row8 < 6
                a1, a2, a3 = split3(jnp.where(live6, lh_ref[t] - centre, 0.0) * scale)
                b1, b2, b3 = split3(jnp.where(live6, rh_ref[t] - centre, 0.0) * scale)
                one = jnp.ones_like(a1)
                left = jnp.concatenate([a1, a2, a3, one, one, one], axis=0).T.astype(bf16)
                diffs = []
                for c in range(6):
                    rhs = jnp.concatenate([unit[c], unit[c], unit[c], -b1 * unit[c], -b2 * unit[c], -b3 * unit[c]], axis=0).astype(bf16)
                    diffs.append(jnp.dot(left, rhs, preferred_element_type=f32))
                dx, dy, dz, du, dv, dw = diffs
                store_forces(t, dx * dx + dy * dy + dz * dz, dx * du + dy * dv + dz * dw, wa, wb)

    @pl.loop(0, MEM_TILES, unroll=UNC)
    def _(t):
        wb = sum_ref[1, t]
        con = lax.dot_general(wb, force_ref[0, t], NT, preferred_element_type=f32) + lax.dot_general(wb, force_ref[1, t], NT, preferred_element_type=f32)
        fo_ref[t, 0:8, :] = (lh_ref[t] - centre_of(range_ref[P_LOW, t])) * con[3:4] - (con[0:8] + con[8:16] + con[16:24])

    @pl.loop(0, MEM_TILES, unroll=UNC)
    def _(t):
        wa = sum_ref[0, t]
        rea = jnp.dot(wa, force_ref[0, t], preferred_element_type=f32) + jnp.dot(wa, force_ref[1, t], preferred_element_type=f32)
        fo_ref[t, 8:16, :] = (rh_ref[t] - centre_of(range_ref[P_LOW, t])) * rea[3:4] - (rea[0:8] + rea[8:16] + rea[16:24])

    def pieces_of(t):
        con, rea = fo_ref[t, 0:8, :], jnp.where(row8 < 3, fo_ref[t, 8:16, :], 0.0)
        c1 = con.astype(bf16).astype(f32)
        r1 = rea.astype(bf16).astype(f32)
        return (c1, con - c1), jnp.concatenate([r1, rea - r1], axis=0).astype(bf16)

    @pl.loop(0, MEM_TILES // UNS)
    def _(part):
        more = jnp.int32(0)
        sums = []
        for k in range(UNS):
            t = part * UNS + k
            con, rea = pieces_of(t)
            vert, index = ver_ref[pl.ds(t, 1), :], par_ref[pl.ds(t, 1), :]
            base = pl.multiple_of((range_ref[V_LOW, t] >> 3) << 3, 8)
            more = jnp.maximum(more, jnp.maximum(range_ref[P_HIGH, t] - range_ref[P_LOW, t], (range_ref[V_HIGH, t] - base) >> 4))
            sums.append((base, vertex_sums(base, vert & 127, vert >> 7, con, rowt, row16),
                         range_ref[P_LOW, t], partner_sums(range_ref[P_LOW, t], index & 127, index >> 7, rea, rowt)))
        for base, con, blk, rea in sums:
            add_vertex(con_ref, base, con)
            add_partner(rea_ref, blk, rea)

        @pl.when(more > 0)
        def _():
            @pl.loop(0, UNS)
            def _(k):
                t = part * UNS + k
                con, rea = pieces_of(t)
                vert, index = ver_ref[pl.ds(t, 1), :], par_ref[pl.ds(t, 1), :]
                base = (range_ref[V_LOW, t] >> 3) << 3

                @pl.loop(1, ((range_ref[V_HIGH, t] - base) >> 4) + 1)
                def _(j):
                    at = pl.multiple_of(base + j * SPAN, 8)
                    add_vertex(con_ref, at, vertex_sums(at, vert & 127, vert >> 7, con, rowt, row16))

                @pl.loop(range_ref[P_LOW, t] + 1, range_ref[P_HIGH, t] + 1)
                def _(blk):
                    add_partner(rea_ref, blk, partner_sums(blk, index & 127, index >> 7, rea, rowt))

    width = out_ref.shape[1]
    for blk in range(-(-width // TILE)):
        at = slice(blk * TILE, min((blk + 1) * TILE, width))
        out_ref[:, at] = vel_ref[:, at] + TIME_STEP * (internal_ref[:, at] + con_ref[:, blk, :at.stop - at.start])

def contact(ranges, tab, mem, internal, vel, vertex, partner, index, count):
    smem, vmem = pl.BlockSpec(memory_space=pltpu.SMEM), pl.BlockSpec(memory_space=pltpu.VMEM)
    tile = pltpu.VMEM((MEM_TILES, 8, TILE), f32)
    return pl.pallas_call(
        contact_kernel,
        out_shape=(
            jax.ShapeDtypeStruct((9 * 3 * BOXES, TILE), f32),
            jax.ShapeDtypeStruct((index.shape[0], 8, TILE), f32),
            jax.ShapeDtypeStruct(vel.shape, f32),
        ),
        in_specs=[smem] * 2 + [vmem] * 7,
        out_specs=(vmem, vmem, vmem),
        scratch_shapes=[pltpu.VMEM((3, MB, TILE), f32), tile, tile, pltpu.VMEM((MEM_TILES, 16, TILE), f32),
                        pltpu.VMEM((2, MEM_TILES, TILE, TILE), bf16), pltpu.VMEM((2, MEM_TILES, 32, TILE), bf16)],
        compiler_params=pltpu.CompilerParams(vmem_limit_bytes=40 * 2**20),
        name="contact",
    )(ranges, count, partner, vertex, index, tab, mem, internal, vel)

BENDING_MODULUS = 20.0
AREA_MODULUS = 40.0

CHUNKS = 3

def block_range(index, unused):
    high = index >> 7
    full = index >= unused
    first = jnp.min(jnp.where(full, (unused >> 7) - 1, high).astype(f32).T, axis=0, keepdims=True)
    last = jnp.max(jnp.where(full, 0, high).astype(f32).T, axis=0, keepdims=True)
    return first.astype(jnp.int32), jnp.maximum(first, last).astype(jnp.int32)

def halo_kernel(nx, ny, pos_ref, vel_ref, mpos_ref, mvel_ref, bend_ref, cell_ref, idx_ref, par_ref, ver_ref,
                tab_ref, mem_ref, internal_ref, range_ref, own_ref, x_ref, send_sem, recv_sem, own_sem):
    gx, gy = lax.axis_index("gx"), lax.axis_index("gy")
    up, down = (lax.rem(gx + 1, nx), gy), (lax.rem(gx + nx - 1, nx), gy)
    right, left = (gx, lax.rem(gy + 1, ny)), (gx, lax.rem(gy + ny - 1, ny))
    size = own_ref.shape[0]
    part = size // CHUNKS

    barrier = pltpu.get_barrier_semaphore()
    for device in (up, down, right, left):
        pl.semaphore_signal(barrier, inc=1, device_id=device, device_id_type=MESH)
    for blk in range(BOXES):
        at = slice(blk * TILE, (blk + 1) * TILE)
        own_ref[pl.ds(blk, 3, stride=BOXES), :] = pos_ref[:, at]
        own_ref[pl.ds(3 * BOXES + blk, 3, stride=BOXES), :] = vel_ref[:, at]
    pl.semaphore_wait(barrier, 4)

    def slot(n, c):
        return tab_ref.at[pl.ds(n * size + c * part, part)]

    def copy(source, n, c, device):
        src = own_ref.at[pl.ds(c * part, part)] if source is None else slot(source, c)
        return pltpu.make_async_remote_copy(
            src_ref=src, dst_ref=slot(n, c), send_sem=send_sem.at[n, c], recv_sem=recv_sem.at[n, c],
            device_id=device, device_id_type=MESH)

    keep = pltpu.make_async_copy(own_ref, tab_ref.at[pl.ds(4 * size, size)], own_sem)
    keep.start()
    first = [[copy(None, 3, c, right), copy(None, 5, c, left)] for c in range(CHUNKS)]
    along = [[copy(None, 1, c, up), copy(None, 7, c, down)] for c in range(CHUNKS)]
    on = [[copy(3, 0, c, up), copy(3, 6, c, down), copy(5, 2, c, up), copy(5, 8, c, down)] for c in range(CHUNKS)]
    for c in range(CHUNKS):
        for one in first[c] + along[c]:
            one.start()

    def forward(c):
        for k in range(2):
            first[c][k].wait_recv()
            on[c][2 * k].start()
            on[c][2 * k + 1].start()

    cells = x_ref.shape[0] // 3
    for d in range(3):
        for j in range(cells):
            x_ref[d * cells + j:d * cells + j + 1, :] = mpos_ref[d:d + 1, j * V:(j + 1) * V]
    x = x_ref[...]
    relative = x - jnp.sum(x, axis=1, keepdims=True) * (1.0 / V)
    once = lax.dot_general(relative, bend_ref[...], NT, precision=lax.Precision.HIGHEST, preferred_element_type=f32)
    forward(0)
    twice = lax.dot_general(once, bend_ref[...], NT, precision=lax.Precision.HIGHEST, preferred_element_type=f32)
    forward(1)
    square = jnp.sum(relative * relative, axis=1, keepdims=True)
    spread = (square[:cells] + square[cells:2 * cells] + square[2 * cells:]) * (1.0 / V)
    stretch = AREA_MODULUS * (spread / cell_ref[:, 0:1] - 1.0)
    alive = cell_ref[:, 1:2]
    for d in range(3):
        rows = slice(d * cells, (d + 1) * cells)
        x_ref[rows] = -(BENDING_MODULUS * twice[rows] + stretch * relative[rows]) * alive
    forward(2)
    for d in range(3):
        for j in range(cells):
            internal_ref[d:d + 1, j * V:(j + 1) * V] = x_ref[d * cells + j:d * cells + j + 1, :]

    width = mpos_ref.shape[1]
    rows = mem_ref.shape[0] // 6
    mem_ref[...] = jnp.zeros_like(mem_ref)
    for blk in range(-(-width // TILE)):
        at = slice(blk * TILE, min((blk + 1) * TILE, width))
        mem_ref[pl.ds(blk, 3, stride=rows), :at.stop - at.start] = mpos_ref[:, at]
        mem_ref[pl.ds(3 * rows + blk, 3, stride=rows), :at.stop - at.start] = mvel_ref[:, at]
    range_ref[...] = jnp.zeros_like(range_ref)
    parts = idx_ref.shape[0] // TILE
    for k in range(parts):
        range_ref[k:k + 1, :], range_ref[parts + k:parts + k + 1, :] = block_range(idx_ref[k * TILE:(k + 1) * TILE, :], 9 * BOXES * TILE)
    for k, ref in ((P_LOW, par_ref), (V_LOW, ver_ref)):
        low, high = block_range(ref[...], 9 * BOXES * TILE)
        range_ref[k:k + 1, :low.shape[1]] = low
        range_ref[k + 1:k + 2, :low.shape[1]] = high
    keep.wait()
    for c in range(CHUNKS):
        for one in first[c]:
            one.wait_send()
        for one in along[c] + on[c]:
            one.wait()

def halo(pos, vel, mpos, mvel, bending, cell, index, partner, vertex):
    size = 6 * BOXES
    nx, ny = lax.axis_size("gx"), lax.axis_size("gy")
    vmem, anywhere = pl.BlockSpec(memory_space=pltpu.VMEM), pl.BlockSpec(memory_space=pl.ANY)
    return pl.pallas_call(
        functools.partial(halo_kernel, nx, ny),
        out_shape=(
            jax.ShapeDtypeStruct((9 * size, TILE), f32),
            jax.ShapeDtypeStruct((6 * MB, TILE), f32),
            jax.ShapeDtypeStruct(mpos.shape, f32),
            jax.ShapeDtypeStruct((16, TILE), jnp.int32),
        ),
        in_specs=[vmem] * 9,
        out_specs=(anywhere, vmem, vmem, vmem),
        scratch_shapes=[pltpu.VMEM((size, TILE), f32), pltpu.VMEM((3 * cell.shape[0], V), f32),
                        pltpu.SemaphoreType.DMA((9, CHUNKS)), pltpu.SemaphoreType.DMA((9, CHUNKS)), pltpu.SemaphoreType.DMA],
        compiler_params=pltpu.CompilerParams(collective_id=0, has_side_effects=True, vmem_limit_bytes=30 * 2**20),
        name="halo",
    )(pos, vel, mpos, mvel, bending, cell, index, partner, vertex)

def on_device(solvent_pos, solvent_vel, pair_index, random_pairs, membrane_pos, membrane_vel, mem_vertex, mem_partner,
              bending, rest_size, cell_count):
    cells = rest_size.shape[0]
    alive = (jnp.arange(cells, dtype=jnp.int32) < cell_count[0]).astype(f32)
    tab, mem, internal, ranges = halo(solvent_pos, solvent_vel, membrane_pos, membrane_vel, bending,
                                      jnp.stack([rest_size, alive], axis=1), pair_index, mem_partner, mem_vertex)
    rea, held, membrane_velocity = contact(ranges, tab, mem, internal, membrane_vel, mem_vertex, mem_partner, pair_index, cell_count)
    solvent_velocity = pairs(held, random_pairs, tab, rea).reshape(3, BOXES * TILE)
    return solvent_velocity, membrane_velocity

def solution(mesh):
    both = ("gx", "gy")
    flat, tiles = P(None, both), P(both, None)
    return jax.shard_map(
        on_device,
        mesh=mesh,
        in_specs=(flat, flat, tiles, P(both, None, None), flat, flat, tiles, tiles, P(), P(both), P(both)),
        out_specs=(flat, flat),
        check_vma=False,
    )
```

```python
import functools
from jax.sharding import PartitionSpec as P
import jax, jax.numpy as jnp
from jax import lax
from jax.experimental import pallas as pl
from jax.experimental.pallas import tpu as pltpu

f32, bf16 = jnp.float32, jnp.bfloat16
BOXES, TILE, PAIRS = 96, 128, 4
GROUP = 16
TIME_STEP = 0.01
SOLVENT_PUSH = 0.5
MESH = pl.DeviceIdType.MESH

def split3(v):
    p1 = v.astype(bf16).astype(f32)
    rest = v - p1
    p2 = rest.astype(bf16).astype(f32)
    return p1, p2, rest - p2

NT = (((1,), (1,)), ((), ()))

def part_of(blk):
    return (blk * 683) >> 16

def row_of(blk):
    return blk + part_of(blk) * (5 * BOXES)

def gather_block(tab_ref, blk, low, high, held, row):
    n = part_of(blk)
    p = (n * 11) >> 5
    dx = (p - 1).astype(f32) * 4.0
    dy = (n - 3 * p - 1).astype(f32) * 4.0
    block = tab_ref[pl.ds(blk + n * (5 * BOXES), 6, stride=BOXES), :]
    got = jnp.take_along_axis(block, low, axis=1, mode="promise_in_bounds")
    got = got + jnp.where(row == 0, dx, jnp.where(row == 1, dy, 0.0))
    return jnp.where(high == blk, got, held)

def box_centre(box, row8):
    cx = (box & 1).astype(f32) * 2.0 + 1.0
    cy = ((box >> 1) & 1).astype(f32) * 2.0 + 1.0
    cz = (box >> 2).astype(f32) * 2.0 + 1.0
    return jnp.where(row8 == 0, cx, jnp.where(row8 == 1, cy, jnp.where(row8 == 2, cz, 0.0)))

def own_features(own, row8, friction):
    a, u = own[0:3], own[3:6] * friction
    aa = jnp.sum(a * a, axis=0, keepdims=True)
    au = jnp.sum(a * u, axis=0, keepdims=True)
    zero = jnp.zeros((3, TILE), f32)
    one = jnp.ones((1, TILE), f32)
    def left(q, const):
        q1, q2, q3 = split3(q)
        c1, c2, c3 = split3(const)
        last = jnp.where(row8 == 0, c1, jnp.where(row8 == 1, c2, jnp.where(row8 == 2, c3, 0.0)))
        return jnp.concatenate([q1, q1, q1, q2, q2, q3, last, jnp.zeros_like(last)], axis=0)
    ql = left(jnp.concatenate([-2.0 * a, zero, one, 0.0 * one], axis=0), aa)
    qs = left(jnp.concatenate([-u, -friction * a, 0.0 * one, friction * one], axis=0), au)
    return jnp.concatenate([ql.T, qs.T], axis=0).astype(bf16)

def right_features(held, centre, row8):
    held = jnp.concatenate([held, held[0:2]], axis=0) - centre
    b, w = held[0:3], held[3:6]
    bb = jnp.sum(b * b, axis=0, keepdims=True)
    bw = jnp.sum(b * w, axis=0, keepdims=True)
    full = jnp.where(row8 == 6, bb, jnp.where(row8 == 7, bw, held))
    p1, p2, p3 = split3(full)
    ones = jnp.ones_like(p1)
    v1 = jnp.where(row8 == 3, 1.0, p1)
    return (jnp.concatenate([p1, p2, p3, p1, p2, p1, ones, ones], axis=0).astype(bf16),
            jnp.concatenate([v1, p2, p3, p3], axis=0).astype(bf16))

def pair_force(out, theta_ref, k, h):
    r2, s = out[:TILE], out[TILE:]
    th = jnp.concatenate([theta_ref[k * PAIRS + 2 * h], theta_ref[k * PAIRS + 2 * h + 1]], axis=1).astype(f32)
    r2 = jnp.maximum(r2, 1e-12)
    q = lax.rsqrt(r2)
    g = jnp.maximum(jnp.minimum(q, 10.0) * (1.0 - r2 * q), 0.0)
    force = g * ((th + 25.0 / 30.0) - g * s)
    fh = force.astype(bf16)
    return fh, (force - fh.astype(f32)).astype(bf16)

def pair_kernel(nx, ny, held_ref, theta_ref, own_ref, rea_ref, out_ref, row_ref, far_ref, back_ref, send_sem, recv_sem, own_sem):
    step = pl.program_id(0)
    row8 = lax.broadcasted_iota(jnp.int32, (8, TILE), 0)
    gx, gy = lax.axis_index("gx"), lax.axis_index("gy")
    size = 3 * BOXES
    down, up = (lax.rem(gx + nx - 1, nx), gy), (lax.rem(gx + 1, nx), gy)
    left, right = (gx, lax.rem(gy + ny - 1, ny)), (gx, lax.rem(gy + 1, ny))

    def send(src, dst, k, device):
        return pltpu.make_async_remote_copy(
            src_ref=src, dst_ref=dst, send_sem=send_sem.at[k], recv_sem=recv_sem.at[k], device_id=device, device_id_type=MESH)

    keep = pltpu.make_async_copy(rea_ref.at[pl.ds(3 * size, 3 * size)], row_ref, own_sem)
    rows = [send(rea_ref.at[pl.ds(0, 3 * size)], far_ref.at[0], 0, down),
            send(rea_ref.at[pl.ds(6 * size, 3 * size)], far_ref.at[1], 1, up)]
    columns = [send(row_ref.at[pl.ds(0, size)], back_ref.at[0], 2, left),
               send(row_ref.at[pl.ds(2 * size, size)], back_ref.at[1], 3, right)]

    @pl.when(step == 0)
    def _():
        barrier = pltpu.get_barrier_semaphore()
        for device in (down, up, left, right):
            pl.semaphore_signal(barrier, inc=1, device_id=device, device_id_type=MESH)
        pl.semaphore_wait(barrier, 4)
        keep.start()
        for one in rows:
            one.start()

    @pl.when(step == BOXES // GROUP // 2)
    def _():
        keep.wait()
        for one in rows:
            one.wait()
        row_ref[...] += far_ref[0] + far_ref[1]
        for one in columns:
            one.start()

    @pl.loop(0, GROUP, unroll=GROUP)
    def _(k):
        box = step * GROUP + k
        centre = box_centre(box, row8)
        own = own_ref[pl.ds(box, 6, stride=BOXES), :] - centre[0:6]
        lhs = own_features(own, row8, 4.5 / 30.0)
        acc = jnp.zeros((32, TILE), f32)
        for h in range(2):
            feats = [right_features(held_ref[k * PAIRS + 2 * h + j, 0:6, :], centre, row8) for j in range(2)]
            rhs, sums = [jnp.concatenate(parts, axis=1) for parts in zip(*feats)]
            out = jnp.dot(lhs, rhs, preferred_element_type=f32)
            for force in pair_force(out, theta_ref, k, h):
                acc += lax.dot_general(sums, force, NT, preferred_element_type=f32)
        out_ref[pl.ds(box, 3, stride=BOXES), :] = 30.0 * (own[0:3] * acc[3:4] - (acc[0:8] + acc[8:16] + acc[16:24])[0:3])

    @pl.when(step == BOXES // GROUP - 1)
    def _():
        for one in columns:
            one.wait()
        total = out_ref[...] + row_ref[pl.ds(size, size), :] + back_ref[0] + back_ref[1]
        row = lax.broadcasted_iota(jnp.int32, (size, TILE), 0)
        total += jnp.where(row < BOXES, SOLVENT_PUSH, 0.0)
        out_ref[...] = own_ref[pl.ds(size, size), :] + TIME_STEP * total

def pairs(held, theta, tab, rea):
    nx, ny = lax.axis_size("gx"), lax.axis_size("gy")
    size = 3 * BOXES
    return pl.pallas_call(
        functools.partial(pair_kernel, nx, ny),
        out_shape=jax.ShapeDtypeStruct((size, TILE), f32),
        grid=(BOXES // GROUP,),
        in_specs=[
            pl.BlockSpec((GROUP * PAIRS, 8, TILE), lambda i: (i, 0, 0)),
            pl.BlockSpec((GROUP * PAIRS, TILE, TILE), lambda i: (i, 0, 0)),
            pl.BlockSpec((2 * size, TILE), lambda i: (4, 0)),
            pl.BlockSpec(memory_space=pl.ANY),
        ],
        out_specs=pl.BlockSpec((size, TILE), lambda i: (0, 0)),
        scratch_shapes=[pltpu.VMEM((3 * size, TILE), f32), pltpu.VMEM((2, 3 * size, TILE), f32), pltpu.VMEM((2, size, TILE), f32),
                        pltpu.SemaphoreType.DMA((4,)), pltpu.SemaphoreType.DMA((4,)), pltpu.SemaphoreType.DMA],
        compiler_params=pltpu.CompilerParams(collective_id=1, has_side_effects=True, vmem_limit_bytes=56 * 2**20),
        name="pairs",
    )(held, theta, tab, rea)


V = 642
MEM_TILES = 64
MB = 96
WIN = 8
SPAN = 16
UNG, UNC, UNS = 16, 8, 16
P_LOW, P_HIGH, V_LOW, V_HIGH = 6, 7, 8, 9

def gather_window(tab_ref, base, low, high, held):
    for k in range(WIN):
        block = tab_ref[pl.ds(base + k, 6, stride=MB), :]
        got = jnp.take_along_axis(block, low, axis=1, mode="promise_in_bounds")
        held = jnp.where(high == base + k, got, held)
    return held

def vertex_sums(base, low, high, pieces, rowt, row16):
    onehot = (rowt == low).astype(f32).astype(bf16)
    hit = high == row16 + base
    left = jnp.concatenate([jnp.where(hit, p[c:c + 1], 0.0) for p in pieces for c in range(3)], axis=0).astype(bf16)
    out = lax.dot_general(left, onehot, NT, preferred_element_type=f32)
    return out[:3 * SPAN] + out[3 * SPAN:]

def add_vertex(con_ref, base, out):
    for c in range(3):
        con_ref[c, pl.ds(base, SPAN), :] += out[c * SPAN:(c + 1) * SPAN]

def partner_sums(blk, low, high, pieces, rowt):
    onehot = ((rowt == low) & (high == blk)).astype(f32).astype(bf16)
    out = lax.dot_general(pieces, onehot, NT, preferred_element_type=f32)
    return (out[0:8] + out[8:16])[0:3]

def add_partner(rea_ref, blk, out):
    rea_ref[pl.ds(blk + part_of(blk) * (2 * BOXES), 3, stride=BOXES), :] += out

def contact_kernel(count, *refs):
    arrays, (rea_ref, held_out_ref, out_ref) = refs[:8], refs[8:11]
    con_ref, held_ref, lh_ref, rh_ref, fo_ref, force_ref, sum_ref, in_sem, out_sem = refs[11:20]
    range_ref, mem_ref, ver_ref, par_ref, idx_ref, tab_ref, internal_ref, vel_ref = local = refs[20:]
    loads = [pltpu.make_async_copy(array, ref, in_sem.at[k]) for k, (array, ref) in enumerate(zip(arrays, local))]
    for load in loads:
        load.start()
    held_copy = pltpu.make_async_copy(held_ref, held_out_ref, out_sem)
    row6 = lax.broadcasted_iota(jnp.int32, (6, TILE), 0)
    row8 = lax.broadcasted_iota(jnp.int32, (8, TILE), 0)
    rowt = lax.broadcasted_iota(jnp.int32, (TILE, TILE), 0)
    row16 = lax.broadcasted_iota(jnp.int32, (SPAN, TILE), 0)
    far = jnp.where(row6 < 3, 1000.0, 0.0)
    alive_end = count[0] * V
    con_ref[...] = jnp.zeros_like(con_ref)
    rea_ref[...] = jnp.zeros_like(rea_ref)
    for load in loads[:6]:
        load.wait()

    @pl.loop(0, idx_ref.shape[0] // UNG)
    def _(part):
        spread = jnp.int32(0)
        for k in range(UNG):
            t = part * UNG + k
            first = range_ref[t >> 7, t & 127]
            spread = jnp.maximum(spread, range_ref[(t >> 7) + 3, t & 127] - first)
            index = jnp.broadcast_to(idx_ref[pl.ds(t, 1), :], (6, TILE))
            held_ref[t, 0:6, :] = gather_block(tab_ref, first, index & 127, index >> 7, far, row6)

        @pl.when(spread > 0)
        def _():
            @pl.loop(0, UNG)
            def _(k):
                t = part * UNG + k
                index = jnp.broadcast_to(idx_ref[pl.ds(t, 1), :], (6, TILE))

                @pl.loop(range_ref[t >> 7, t & 127] + 1, range_ref[(t >> 7) + 3, t & 127] + 1)
                def _(blk):
                    held_ref[t, 0:6, :] = gather_block(tab_ref, blk, index & 127, index >> 7, held_ref[t, 0:6, :], row6)

    held_copy.start()

    @pl.loop(0, MEM_TILES // UNG)
    def _(part):
        spread = jnp.int32(0)
        vspread = jnp.int32(0)
        for k in range(UNG):
            t = part * UNG + k
            first = range_ref[P_LOW, t]
            spread = jnp.maximum(spread, range_ref[P_HIGH, t] - first)
            vspread = jnp.maximum(vspread, range_ref[V_HIGH, t] - range_ref[V_LOW, t])
            index = jnp.broadcast_to(par_ref[pl.ds(t, 1), :], (6, TILE))
            rh_ref[t, 0:6, :] = gather_block(tab_ref, first, index & 127, index >> 7, far, row6)
            vert = jnp.broadcast_to(ver_ref[pl.ds(t, 1), :], (6, TILE))
            high = jnp.where(vert < alive_end, vert >> 7, -1)
            lh_ref[t, 0:6, :] = gather_window(mem_ref, range_ref[V_LOW, t], vert & 127, high, far)

        @pl.when(spread > 0)
        def _():
            @pl.loop(0, UNG)
            def _(k):
                t = part * UNG + k
                index = jnp.broadcast_to(par_ref[pl.ds(t, 1), :], (6, TILE))

                @pl.loop(range_ref[P_LOW, t] + 1, range_ref[P_HIGH, t] + 1)
                def _(blk):
                    rh_ref[t, 0:6, :] = gather_block(tab_ref, blk, index & 127, index >> 7, rh_ref[t, 0:6, :], row6)

        @pl.when(vspread >= WIN)
        def _():
            @pl.loop(0, UNG)
            def _(k):
                t = part * UNG + k
                vert = jnp.broadcast_to(ver_ref[pl.ds(t, 1), :], (6, TILE))
                high = jnp.where(vert < alive_end, vert >> 7, -1)

                @pl.loop(1, (range_ref[V_HIGH, t] - range_ref[V_LOW, t]) // WIN + 1)
                def _(j):
                    lh_ref[t, 0:6, :] = gather_window(mem_ref, range_ref[V_LOW, t] + j * WIN, vert & 127, high, lh_ref[t, 0:6, :])

    def centre_of(blk):
        n = part_of(blk)
        box = blk - BOXES * n
        p = (n * 11) >> 5
        cx = ((p - 1) * 4 + (box & 1) * 2 + 1).astype(f32)
        cy = ((n - 3 * p - 1) * 4 + ((box >> 1) & 1) * 2 + 1).astype(f32)
        cz = ((box >> 2) * 2 + 1).astype(f32)
        return jnp.where(row8 == 0, cx, jnp.where(row8 == 1, cy, jnp.where(row8 == 2, cz, 0.0)))

    def store_forces(t, r2, s, wa, wb):
        r2 = jnp.maximum(r2, 1e-12)
        q = lax.rsqrt(r2)
        g = jnp.maximum(jnp.minimum(q, 10.0) * (1.0 - r2 * q), 0.0)
        force = g * (25.0 - g * s)
        force_ref[0, t] = force.astype(bf16)
        force_ref[1, t] = (force - force_ref[0, t].astype(f32)).astype(bf16)
        sum_ref[0, t] = wa
        sum_ref[1, t] = wb

    unit = [jnp.where(row8 == c, 1.0, 0.0) for c in range(6)]
    scale = jnp.where(row8 < 3, 1.0, 4.5)

    @pl.loop(0, MEM_TILES // UNC)
    def _(part):
        spread = jnp.int32(0)
        for k in range(UNC):
            t = part * UNC + k
            spread = jnp.maximum(spread, range_ref[P_HIGH, t] - range_ref[P_LOW, t])
            centre = centre_of(range_ref[P_LOW, t])
            left, right = lh_ref[t, 0:6, :], rh_ref[t, 0:6, :]
            lhs = own_features(left - centre[0:6], row8, 4.5)
            rhs, wb = right_features(right, centre, row8)
            wa = right_features(left, centre, row8)[1]
            out = jnp.dot(lhs, rhs, preferred_element_type=f32)
            store_forces(t, out[:TILE], out[TILE:], wa, wb)

        @pl.when(spread > 0)
        def _():
            @pl.loop(0, UNC)
            def _(k):
                t = part * UNC + k
                centre = centre_of(range_ref[P_LOW, t])
                left, right = lh_ref[t, 0:6, :], rh_ref[t, 0:6, :]
                wb, wa = right_features(right, centre, row8)[1], right_features(left, centre, row8)[1]
                live6 = row8 < 6
                a1, a2, a3 = split3(jnp.where(live6, lh_ref[t] - centre, 0.0) * scale)
                b1, b2, b3 = split3(jnp.where(live6, rh_ref[t] - centre, 0.0) * scale)
                one = jnp.ones_like(a1)
                left = jnp.concatenate([a1, a2, a3, one, one, one], axis=0).T.astype(bf16)
                diffs = []
                for c in range(6):
                    rhs = jnp.concatenate([unit[c], unit[c], unit[c], -b1 * unit[c], -b2 * unit[c], -b3 * unit[c]], axis=0).astype(bf16)
                    diffs.append(jnp.dot(left, rhs, preferred_element_type=f32))
                dx, dy, dz, du, dv, dw = diffs
                store_forces(t, dx * dx + dy * dy + dz * dz, dx * du + dy * dv + dz * dw, wa, wb)

    @pl.loop(0, MEM_TILES, unroll=UNC)
    def _(t):
        wb = sum_ref[1, t]
        con = lax.dot_general(wb, force_ref[0, t], NT, preferred_element_type=f32) + lax.dot_general(wb, force_ref[1, t], NT, preferred_element_type=f32)
        fo_ref[t, 0:8, :] = (lh_ref[t] - centre_of(range_ref[P_LOW, t])) * con[3:4] - (con[0:8] + con[8:16] + con[16:24])

    @pl.loop(0, MEM_TILES, unroll=UNC)
    def _(t):
        wa = sum_ref[0, t]
        rea = jnp.dot(wa, force_ref[0, t], preferred_element_type=f32) + jnp.dot(wa, force_ref[1, t], preferred_element_type=f32)
        fo_ref[t, 8:16, :] = (rh_ref[t] - centre_of(range_ref[P_LOW, t])) * rea[3:4] - (rea[0:8] + rea[8:16] + rea[16:24])

    def pieces_of(t):
        con, rea = fo_ref[t, 0:8, :], jnp.where(row8 < 3, fo_ref[t, 8:16, :], 0.0)
        c1 = con.astype(bf16).astype(f32)
        r1 = rea.astype(bf16).astype(f32)
        return (c1, con - c1), jnp.concatenate([r1, rea - r1], axis=0).astype(bf16)

    @pl.loop(0, MEM_TILES // UNS)
    def _(part):
        more = jnp.int32(0)
        sums = []
        for k in range(UNS):
            t = part * UNS + k
            con, rea = pieces_of(t)
            vert, index = ver_ref[pl.ds(t, 1), :], par_ref[pl.ds(t, 1), :]
            base = pl.multiple_of((range_ref[V_LOW, t] >> 3) << 3, 8)
            more = jnp.maximum(more, jnp.maximum(range_ref[P_HIGH, t] - range_ref[P_LOW, t], (range_ref[V_HIGH, t] - base) >> 4))
            sums.append((base, vertex_sums(base, vert & 127, vert >> 7, con, rowt, row16),
                         range_ref[P_LOW, t], partner_sums(range_ref[P_LOW, t], index & 127, index >> 7, rea, rowt)))
        for base, con, blk, rea in sums:
            add_vertex(con_ref, base, con)
            add_partner(rea_ref, blk, rea)

        @pl.when(more > 0)
        def _():
            @pl.loop(0, UNS)
            def _(k):
                t = part * UNS + k
                con, rea = pieces_of(t)
                vert, index = ver_ref[pl.ds(t, 1), :], par_ref[pl.ds(t, 1), :]
                base = (range_ref[V_LOW, t] >> 3) << 3

                @pl.loop(1, ((range_ref[V_HIGH, t] - base) >> 4) + 1)
                def _(j):
                    at = pl.multiple_of(base + j * SPAN, 8)
                    add_vertex(con_ref, at, vertex_sums(at, vert & 127, vert >> 7, con, rowt, row16))

                @pl.loop(range_ref[P_LOW, t] + 1, range_ref[P_HIGH, t] + 1)
                def _(blk):
                    add_partner(rea_ref, blk, partner_sums(blk, index & 127, index >> 7, rea, rowt))

    for load in loads[6:]:
        load.wait()
    width = out_ref.shape[1]
    for blk in range(-(-width // TILE)):
        at = slice(blk * TILE, min((blk + 1) * TILE, width))
        out_ref[:, at] = vel_ref[:, at] + TIME_STEP * (internal_ref[:, at] + con_ref[:, blk, :at.stop - at.start])
    held_copy.wait()

def contact(ranges, tab, mem, internal, vel, vertex, partner, index, count):
    arrays = ranges, mem, vertex, partner, index, tab, internal, vel
    hbm, vmem = pl.BlockSpec(memory_space=pltpu.HBM), pl.BlockSpec(memory_space=pltpu.VMEM)
    tile = pltpu.VMEM((MEM_TILES, 8, TILE), f32)
    held = jax.ShapeDtypeStruct((index.shape[0], 8, TILE), f32)
    return pl.pallas_call(
        contact_kernel,
        out_shape=(jax.ShapeDtypeStruct((9 * 3 * BOXES, TILE), f32), held, jax.ShapeDtypeStruct(vel.shape, f32)),
        in_specs=[pl.BlockSpec(memory_space=pltpu.SMEM)] + [hbm] * 8,
        out_specs=(vmem, hbm, vmem),
        scratch_shapes=[pltpu.VMEM((3, MB, TILE), f32), pltpu.VMEM(held.shape, f32), tile, tile, pltpu.VMEM((MEM_TILES, 16, TILE), f32),
                        pltpu.VMEM((2, MEM_TILES, TILE, TILE), bf16), pltpu.VMEM((2, MEM_TILES, 32, TILE), bf16),
                        pltpu.SemaphoreType.DMA((8,)), pltpu.SemaphoreType.DMA, pltpu.SMEM(ranges.shape, ranges.dtype)]
        + [pltpu.VMEM(x.shape, x.dtype) for x in arrays[1:]],
        compiler_params=pltpu.CompilerParams(vmem_limit_bytes=56 * 2**20),
        name="contact",
    )(count, *arrays)

BENDING_MODULUS = 20.0
AREA_MODULUS = 40.0

CHUNKS = 3

def block_range(index, unused):
    high = index >> 7
    full = index >= unused
    first = jnp.min(jnp.where(full, (unused >> 7) - 1, high).astype(f32).T, axis=0, keepdims=True)
    last = jnp.max(jnp.where(full, 0, high).astype(f32).T, axis=0, keepdims=True)
    return first.astype(jnp.int32), jnp.maximum(first, last).astype(jnp.int32)

def halo_kernel(nx, ny, *refs):
    arrays, (rest_ref, count_ref, tab_ref, mem_ref, internal_ref, range_ref) = refs[:8], refs[8:14]
    own_ref, x_ref, send_sem, recv_sem, own_sem, in_sem = refs[14:20]
    pos_ref, vel_ref, mpos_ref, mvel_ref, bend_ref, idx_ref, par_ref, ver_ref = local = refs[20:]
    gx, gy = lax.axis_index("gx"), lax.axis_index("gy")
    up, down = (lax.rem(gx + 1, nx), gy), (lax.rem(gx + nx - 1, nx), gy)
    right, left = (gx, lax.rem(gy + 1, ny)), (gx, lax.rem(gy + ny - 1, ny))
    size = own_ref.shape[0]
    part = size // CHUNKS

    barrier = pltpu.get_barrier_semaphore()
    for device in (up, down, right, left):
        pl.semaphore_signal(barrier, inc=1, device_id=device, device_id_type=MESH)
    loads = [pltpu.make_async_copy(array, ref, in_sem.at[k]) for k, (array, ref) in enumerate(zip(arrays, local))]
    for load in loads:
        load.start()
    loads[0].wait()
    loads[1].wait()
    for blk in range(BOXES):
        at = slice(blk * TILE, (blk + 1) * TILE)
        own_ref[pl.ds(blk, 3, stride=BOXES), :] = pos_ref[:, at]
        own_ref[pl.ds(3 * BOXES + blk, 3, stride=BOXES), :] = vel_ref[:, at]
    pl.semaphore_wait(barrier, 4)

    def slot(n, c):
        return tab_ref.at[pl.ds(n * size + c * part, part)]

    def copy(source, n, c, device):
        src = own_ref.at[pl.ds(c * part, part)] if source is None else slot(source, c)
        return pltpu.make_async_remote_copy(
            src_ref=src, dst_ref=slot(n, c), send_sem=send_sem.at[n, c], recv_sem=recv_sem.at[n, c],
            device_id=device, device_id_type=MESH)

    keep = pltpu.make_async_copy(own_ref, tab_ref.at[pl.ds(4 * size, size)], own_sem)
    keep.start()
    first = [[copy(None, 3, c, right), copy(None, 5, c, left)] for c in range(CHUNKS)]
    along = [[copy(None, 1, c, up), copy(None, 7, c, down)] for c in range(CHUNKS)]
    on = [[copy(3, 0, c, up), copy(3, 6, c, down), copy(5, 2, c, up), copy(5, 8, c, down)] for c in range(CHUNKS)]
    for c in range(CHUNKS):
        for one in first[c] + along[c]:
            one.start()

    def forward(c):
        for k in range(2):
            first[c][k].wait_recv()
            on[c][2 * k].start()
            on[c][2 * k + 1].start()

    for load in loads[2:]:
        load.wait()
    cells = x_ref.shape[0] // 3
    for d in range(3):
        for j in range(cells):
            x_ref[d * cells + j:d * cells + j + 1, :] = mpos_ref[d:d + 1, j * V:(j + 1) * V]
    x = x_ref[...]
    relative = x - jnp.sum(x, axis=1, keepdims=True) * (1.0 / V)
    once = lax.dot_general(relative, bend_ref[...], NT, precision=lax.Precision.HIGHEST, preferred_element_type=f32)
    forward(0)
    twice = lax.dot_general(once, bend_ref[...], NT, precision=lax.Precision.HIGHEST, preferred_element_type=f32)
    forward(1)
    square = jnp.sum(relative * relative, axis=1, keepdims=True)
    spread = (square[:cells] + square[cells:2 * cells] + square[2 * cells:]) * (1.0 / V)
    slot_row = lax.broadcasted_iota(jnp.int32, (cells, 1), 0)
    rest = jnp.ones((cells, 1), f32)
    for j in range(cells):
        rest = jnp.where(slot_row == j, rest_ref[j], rest)
    stretch = AREA_MODULUS * (spread / rest - 1.0)
    alive = (slot_row < count_ref[0]).astype(f32)
    for d in range(3):
        rows = slice(d * cells, (d + 1) * cells)
        x_ref[rows] = -(BENDING_MODULUS * twice[rows] + stretch * relative[rows]) * alive
    forward(2)
    for d in range(3):
        for j in range(cells):
            internal_ref[d:d + 1, j * V:(j + 1) * V] = x_ref[d * cells + j:d * cells + j + 1, :]

    width = mpos_ref.shape[1]
    rows = mem_ref.shape[0] // 6
    mem_ref[...] = jnp.zeros_like(mem_ref)
    for blk in range(-(-width // TILE)):
        at = slice(blk * TILE, min((blk + 1) * TILE, width))
        mem_ref[pl.ds(blk, 3, stride=rows), :at.stop - at.start] = mpos_ref[:, at]
        mem_ref[pl.ds(3 * rows + blk, 3, stride=rows), :at.stop - at.start] = mvel_ref[:, at]
    range_ref[...] = jnp.zeros_like(range_ref)
    parts = idx_ref.shape[0] // TILE
    for k in range(parts):
        range_ref[k:k + 1, :], range_ref[parts + k:parts + k + 1, :] = block_range(idx_ref[k * TILE:(k + 1) * TILE, :], 9 * BOXES * TILE)
    for k, ref in ((P_LOW, par_ref), (V_LOW, ver_ref)):
        low, high = block_range(ref[...], 9 * BOXES * TILE)
        range_ref[k:k + 1, :low.shape[1]] = low
        range_ref[k + 1:k + 2, :low.shape[1]] = high
    keep.wait()
    for c in range(CHUNKS):
        for one in first[c]:
            one.wait_send()
        for one in along[c] + on[c]:
            one.wait()

def halo(pos, vel, mpos, mvel, bending, index, partner, vertex, rest, count):
    size = 6 * BOXES
    arrays = pos, vel, mpos, mvel, bending, index, partner, vertex
    nx, ny = lax.axis_size("gx"), lax.axis_size("gy")
    vmem, anywhere = pl.BlockSpec(memory_space=pltpu.VMEM), pl.BlockSpec(memory_space=pl.ANY)
    return pl.pallas_call(
        functools.partial(halo_kernel, nx, ny),
        out_shape=(
            jax.ShapeDtypeStruct((9 * size, TILE), f32),
            jax.ShapeDtypeStruct((6 * MB, TILE), f32),
            jax.ShapeDtypeStruct(mpos.shape, f32),
            jax.ShapeDtypeStruct((16, TILE), jnp.int32),
        ),
        in_specs=[pl.BlockSpec(memory_space=pltpu.HBM)] * 8 + [pl.BlockSpec(memory_space=pltpu.SMEM)] * 2,
        out_specs=(anywhere, vmem, vmem, vmem),
        scratch_shapes=[pltpu.VMEM((size, TILE), f32), pltpu.VMEM((3 * rest.shape[0], V), f32),
                        pltpu.SemaphoreType.DMA((9, CHUNKS)), pltpu.SemaphoreType.DMA((9, CHUNKS)), pltpu.SemaphoreType.DMA,
                        pltpu.SemaphoreType.DMA((8,))] + [pltpu.VMEM(x.shape, x.dtype) for x in arrays],
        compiler_params=pltpu.CompilerParams(collective_id=0, has_side_effects=True, vmem_limit_bytes=56 * 2**20),
        name="halo",
    )(*arrays, rest, count)

def on_device(solvent_pos, solvent_vel, pair_index, random_pairs, membrane_pos, membrane_vel, mem_vertex, mem_partner,
              bending, rest_size, cell_count):
    tab, mem, internal, ranges = halo(solvent_pos, solvent_vel, membrane_pos, membrane_vel, bending, pair_index, mem_partner,
                                      mem_vertex, rest_size, cell_count)
    rea, held, membrane_velocity = contact(ranges, tab, mem, internal, membrane_vel, mem_vertex, mem_partner, pair_index, cell_count)
    solvent_velocity = pairs(held, random_pairs, tab, rea).reshape(3, BOXES * TILE)
    return solvent_velocity, membrane_velocity

def solution(mesh):
    both = ("gx", "gy")
    flat, tiles = P(None, both), P(both, None)
    return jax.shard_map(
        on_device,
        mesh=mesh,
        in_specs=(flat, flat, tiles, P(both, None, None), flat, flat, tiles, tiles, P(), P(both), P(both)),
        out_specs=(flat, flat),
        check_vma=False,
    )
```

```python
import functools
from jax.sharding import PartitionSpec as P
import jax, jax.numpy as jnp
from jax import lax
from jax.experimental import pallas as pl
from jax.experimental.pallas import tpu as pltpu

f32, bf16 = jnp.float32, jnp.bfloat16
BOXES, TILE, PAIRS = 96, 128, 4
GROUP = 16
TIME_STEP = 0.01
SOLVENT_PUSH = 0.5
MESH = pl.DeviceIdType.MESH

def split3(v):
    p1 = v.astype(bf16).astype(f32)
    rest = v - p1
    p2 = rest.astype(bf16).astype(f32)
    return p1, p2, rest - p2

NT = (((1,), (1,)), ((), ()))

def part_of(blk):
    return (blk * 683) >> 16

def row_of(blk):
    return blk + part_of(blk) * (5 * BOXES)

def gather_block(tab_ref, blk, low, high, held, row):
    n = part_of(blk)
    p = (n * 11) >> 5
    dx = (p - 1).astype(f32) * 4.0
    dy = (n - 3 * p - 1).astype(f32) * 4.0
    block = tab_ref[pl.ds(blk + n * (5 * BOXES), 6, stride=BOXES), :]
    got = jnp.take_along_axis(block, low, axis=1, mode="promise_in_bounds")
    got = got + jnp.where(row == 0, dx, jnp.where(row == 1, dy, 0.0))
    return jnp.where(high == blk, got, held)

def box_centre(box, row8):
    cx = (box & 1).astype(f32) * 2.0 + 1.0
    cy = ((box >> 1) & 1).astype(f32) * 2.0 + 1.0
    cz = (box >> 2).astype(f32) * 2.0 + 1.0
    return jnp.where(row8 == 0, cx, jnp.where(row8 == 1, cy, jnp.where(row8 == 2, cz, 0.0)))

def own_features(own, row8, friction):
    a, u = own[0:3], own[3:6] * friction
    aa = jnp.sum(a * a, axis=0, keepdims=True)
    au = jnp.sum(a * u, axis=0, keepdims=True)
    zero = jnp.zeros((3, TILE), f32)
    one = jnp.ones((1, TILE), f32)
    def left(q, const):
        q1, q2, q3 = split3(q)
        c1, c2, c3 = split3(const)
        last = jnp.where(row8 == 0, c1, jnp.where(row8 == 1, c2, jnp.where(row8 == 2, c3, 0.0)))
        return jnp.concatenate([q1, q1, q1, q2, q2, q3, last, jnp.zeros_like(last)], axis=0)
    ql = left(jnp.concatenate([-2.0 * a, zero, one, 0.0 * one], axis=0), aa)
    qs = left(jnp.concatenate([-u, -friction * a, 0.0 * one, friction * one], axis=0), au)
    return jnp.concatenate([ql.T, qs.T], axis=0).astype(bf16)

def right_features(held, centre, row8):
    held = jnp.concatenate([held, held[0:2]], axis=0) - centre
    b, w = held[0:3], held[3:6]
    bb = jnp.sum(b * b, axis=0, keepdims=True)
    bw = jnp.sum(b * w, axis=0, keepdims=True)
    full = jnp.where(row8 == 6, bb, jnp.where(row8 == 7, bw, held))
    p1, p2, p3 = split3(full)
    ones = jnp.ones_like(p1)
    v1 = jnp.where(row8 == 3, 1.0, p1)
    return (jnp.concatenate([p1, p2, p3, p1, p2, p1, ones, ones], axis=0).astype(bf16),
            jnp.concatenate([v1, p2, p3, p3], axis=0).astype(bf16))

def pair_force(out, theta_ref, k, h):
    r2, s = out[:TILE], out[TILE:]
    th = jnp.concatenate([theta_ref[k * PAIRS + 2 * h], theta_ref[k * PAIRS + 2 * h + 1]], axis=1).astype(f32)
    r2 = jnp.maximum(r2, 1e-12)
    q = lax.rsqrt(r2)
    g = jnp.maximum(jnp.minimum(q, 10.0) * (1.0 - r2 * q), 0.0)
    force = g * ((th + 25.0 / 30.0) - g * s)
    fh = force.astype(bf16)
    return fh, (force - fh.astype(f32)).astype(bf16)

def pair_kernel(nx, ny, held_ref, theta_ref, own_ref, rea_ref, out_ref, row_ref, far_ref, back_ref, send_sem, recv_sem, own_sem):
    step = pl.program_id(0)
    row8 = lax.broadcasted_iota(jnp.int32, (8, TILE), 0)
    gx, gy = lax.axis_index("gx"), lax.axis_index("gy")
    size = 3 * BOXES
    down, up = (lax.rem(gx + nx - 1, nx), gy), (lax.rem(gx + 1, nx), gy)
    left, right = (gx, lax.rem(gy + ny - 1, ny)), (gx, lax.rem(gy + 1, ny))

    def send(src, dst, k, device):
        return pltpu.make_async_remote_copy(
            src_ref=src, dst_ref=dst, send_sem=send_sem.at[k], recv_sem=recv_sem.at[k], device_id=device, device_id_type=MESH)

    keep = pltpu.make_async_copy(rea_ref.at[pl.ds(3 * size, 3 * size)], row_ref, own_sem)
    rows = [send(rea_ref.at[pl.ds(0, 3 * size)], far_ref.at[0], 0, down),
            send(rea_ref.at[pl.ds(6 * size, 3 * size)], far_ref.at[1], 1, up)]
    columns = [send(row_ref.at[pl.ds(0, size)], back_ref.at[0], 2, left),
               send(row_ref.at[pl.ds(2 * size, size)], back_ref.at[1], 3, right)]

    @pl.when(step == 0)
    def _():
        barrier = pltpu.get_barrier_semaphore()
        for device in (down, up, left, right):
            pl.semaphore_signal(barrier, inc=1, device_id=device, device_id_type=MESH)
        pl.semaphore_wait(barrier, 4)
        keep.start()
        for one in rows:
            one.start()

    @pl.when(step == BOXES // GROUP // 2)
    def _():
        keep.wait()
        for one in rows:
            one.wait()
        row_ref[...] += far_ref[0] + far_ref[1]
        for one in columns:
            one.start()

    @pl.loop(0, GROUP, unroll=GROUP)
    def _(k):
        box = step * GROUP + k
        centre = box_centre(box, row8)
        own = own_ref[pl.ds(box, 6, stride=BOXES), :] - centre[0:6]
        lhs = own_features(own, row8, 4.5 / 30.0)
        acc = jnp.zeros((32, TILE), f32)
        for h in range(2):
            feats = [right_features(held_ref[k * PAIRS + 2 * h + j, 0:6, :], centre, row8) for j in range(2)]
            rhs, sums = [jnp.concatenate(parts, axis=1) for parts in zip(*feats)]
            out = jnp.dot(lhs, rhs, preferred_element_type=f32)
            for force in pair_force(out, theta_ref, k, h):
                acc += lax.dot_general(sums, force, NT, preferred_element_type=f32)
        out_ref[pl.ds(box, 3, stride=BOXES), :] = 30.0 * (own[0:3] * acc[3:4] - (acc[0:8] + acc[8:16] + acc[16:24])[0:3])

    @pl.when(step == BOXES // GROUP - 1)
    def _():
        for one in columns:
            one.wait()
        total = out_ref[...] + row_ref[pl.ds(size, size), :] + back_ref[0] + back_ref[1]
        row = lax.broadcasted_iota(jnp.int32, (size, TILE), 0)
        total += jnp.where(row < BOXES, SOLVENT_PUSH, 0.0)
        out_ref[...] = own_ref[pl.ds(size, size), :] + TIME_STEP * total

def pairs(held, theta, tab, rea):
    nx, ny = lax.axis_size("gx"), lax.axis_size("gy")
    size = 3 * BOXES
    return pl.pallas_call(
        functools.partial(pair_kernel, nx, ny),
        out_shape=jax.ShapeDtypeStruct((size, TILE), f32),
        grid=(BOXES // GROUP,),
        in_specs=[
            pl.BlockSpec((GROUP * PAIRS, 8, TILE), lambda i: (i, 0, 0)),
            pl.BlockSpec((GROUP * PAIRS, TILE, TILE), lambda i: (i, 0, 0)),
            pl.BlockSpec((2 * size, TILE), lambda i: (4, 0)),
            pl.BlockSpec(memory_space=pl.ANY),
        ],
        out_specs=pl.BlockSpec((size, TILE), lambda i: (0, 0)),
        scratch_shapes=[pltpu.VMEM((3 * size, TILE), f32), pltpu.VMEM((2, 3 * size, TILE), f32), pltpu.VMEM((2, size, TILE), f32),
                        pltpu.SemaphoreType.DMA((4,)), pltpu.SemaphoreType.DMA((4,)), pltpu.SemaphoreType.DMA],
        compiler_params=pltpu.CompilerParams(collective_id=1, has_side_effects=True, vmem_limit_bytes=56 * 2**20),
        name="pairs",
    )(held, theta, tab, rea)


V = 642
MEM_TILES = 64
MB = 96
WIN = 8
SPAN = 16
UNG, UNC, UNS = 32, 16, 32
P_LOW, P_HIGH, V_LOW, V_HIGH = 6, 7, 8, 9

def gather_window(tab_ref, base, low, high, held):
    for k in range(WIN):
        block = tab_ref[pl.ds(base + k, 6, stride=MB), :]
        got = jnp.take_along_axis(block, low, axis=1, mode="promise_in_bounds")
        held = jnp.where(high == base + k, got, held)
    return held

def vertex_sums(base, low, high, pieces, rowt, row16):
    onehot = (rowt == low).astype(f32).astype(bf16)
    hit = high == row16 + base
    left = jnp.concatenate([jnp.where(hit, p[c:c + 1], 0.0) for p in pieces for c in range(3)], axis=0).astype(bf16)
    out = lax.dot_general(left, onehot, NT, preferred_element_type=f32)
    return out[:3 * SPAN] + out[3 * SPAN:]

def add_vertex(con_ref, base, out):
    for c in range(3):
        con_ref[c, pl.ds(base, SPAN), :] += out[c * SPAN:(c + 1) * SPAN]

def partner_sums(blk, low, high, pieces, rowt):
    onehot = ((rowt == low) & (high == blk)).astype(f32).astype(bf16)
    out = lax.dot_general(pieces, onehot, NT, preferred_element_type=f32)
    return (out[0:8] + out[8:16])[0:3]

def add_partner(rea_ref, blk, out):
    rea_ref[pl.ds(blk + part_of(blk) * (2 * BOXES), 3, stride=BOXES), :] += out

def contact_kernel(count, *refs):
    arrays, (rea_ref, held_out_ref, out_ref) = refs[:8], refs[8:11]
    con_ref, held_ref, lh_ref, rh_ref, fo_ref, force_ref, sum_ref, in_sem, out_sem = refs[11:20]
    range_ref, mem_ref, ver_ref, par_ref, idx_ref, tab_ref, internal_ref, vel_ref = local = refs[20:]
    loads = [pltpu.make_async_copy(array, ref, in_sem.at[k]) for k, (array, ref) in enumerate(zip(arrays, local))]
    for load in loads:
        load.start()
    held_copy = pltpu.make_async_copy(held_ref, held_out_ref, out_sem)
    row6 = lax.broadcasted_iota(jnp.int32, (6, TILE), 0)
    row8 = lax.broadcasted_iota(jnp.int32, (8, TILE), 0)
    rowt = lax.broadcasted_iota(jnp.int32, (TILE, TILE), 0)
    row16 = lax.broadcasted_iota(jnp.int32, (SPAN, TILE), 0)
    far = jnp.where(row6 < 3, 1000.0, 0.0)
    alive_end = count[0] * V
    con_ref[...] = jnp.zeros_like(con_ref)
    rea_ref[...] = jnp.zeros_like(rea_ref)
    for load in loads[:6]:
        load.wait()

    @pl.loop(0, idx_ref.shape[0] // UNG)
    def _(part):
        spread = jnp.int32(0)
        for k in range(UNG):
            t = part * UNG + k
            first = range_ref[t >> 7, t & 127]
            spread = jnp.maximum(spread, range_ref[(t >> 7) + 3, t & 127] - first)
            index = jnp.broadcast_to(idx_ref[pl.ds(t, 1), :], (6, TILE))
            held_ref[t, 0:6, :] = gather_block(tab_ref, first, index & 127, index >> 7, far, row6)

        @pl.when(spread > 0)
        def _():
            @pl.loop(0, UNG)
            def _(k):
                t = part * UNG + k
                index = jnp.broadcast_to(idx_ref[pl.ds(t, 1), :], (6, TILE))

                @pl.loop(range_ref[t >> 7, t & 127] + 1, range_ref[(t >> 7) + 3, t & 127] + 1)
                def _(blk):
                    held_ref[t, 0:6, :] = gather_block(tab_ref, blk, index & 127, index >> 7, held_ref[t, 0:6, :], row6)

    held_copy.start()

    @pl.loop(0, MEM_TILES // UNG)
    def _(part):
        spread = jnp.int32(0)
        vspread = jnp.int32(0)
        for k in range(UNG):
            t = part * UNG + k
            first = range_ref[P_LOW, t]
            spread = jnp.maximum(spread, range_ref[P_HIGH, t] - first)
            vspread = jnp.maximum(vspread, range_ref[V_HIGH, t] - range_ref[V_LOW, t])
            index = jnp.broadcast_to(par_ref[pl.ds(t, 1), :], (6, TILE))
            rh_ref[t, 0:6, :] = gather_block(tab_ref, first, index & 127, index >> 7, far, row6)
            vert = jnp.broadcast_to(ver_ref[pl.ds(t, 1), :], (6, TILE))
            high = jnp.where(vert < alive_end, vert >> 7, -1)
            lh_ref[t, 0:6, :] = gather_window(mem_ref, range_ref[V_LOW, t], vert & 127, high, far)

        @pl.when(spread > 0)
        def _():
            @pl.loop(0, UNG)
            def _(k):
                t = part * UNG + k
                index = jnp.broadcast_to(par_ref[pl.ds(t, 1), :], (6, TILE))

                @pl.loop(range_ref[P_LOW, t] + 1, range_ref[P_HIGH, t] + 1)
                def _(blk):
                    rh_ref[t, 0:6, :] = gather_block(tab_ref, blk, index & 127, index >> 7, rh_ref[t, 0:6, :], row6)

        @pl.when(vspread >= WIN)
        def _():
            @pl.loop(0, UNG)
            def _(k):
                t = part * UNG + k
                vert = jnp.broadcast_to(ver_ref[pl.ds(t, 1), :], (6, TILE))
                high = jnp.where(vert < alive_end, vert >> 7, -1)

                @pl.loop(1, (range_ref[V_HIGH, t] - range_ref[V_LOW, t]) // WIN + 1)
                def _(j):
                    lh_ref[t, 0:6, :] = gather_window(mem_ref, range_ref[V_LOW, t] + j * WIN, vert & 127, high, lh_ref[t, 0:6, :])

    def centre_of(blk):
        n = part_of(blk)
        box = blk - BOXES * n
        p = (n * 11) >> 5
        cx = ((p - 1) * 4 + (box & 1) * 2 + 1).astype(f32)
        cy = ((n - 3 * p - 1) * 4 + ((box >> 1) & 1) * 2 + 1).astype(f32)
        cz = ((box >> 2) * 2 + 1).astype(f32)
        return jnp.where(row8 == 0, cx, jnp.where(row8 == 1, cy, jnp.where(row8 == 2, cz, 0.0)))

    def store_forces(t, r2, s, wa, wb):
        r2 = jnp.maximum(r2, 1e-12)
        q = lax.rsqrt(r2)
        g = jnp.maximum(jnp.minimum(q, 10.0) * (1.0 - r2 * q), 0.0)
        force = g * (25.0 - g * s)
        force_ref[0, t] = force.astype(bf16)
        force_ref[1, t] = (force - force_ref[0, t].astype(f32)).astype(bf16)
        sum_ref[0, t] = wa
        sum_ref[1, t] = wb

    unit = [jnp.where(row8 == c, 1.0, 0.0) for c in range(6)]
    scale = jnp.where(row8 < 3, 1.0, 4.5)

    @pl.loop(0, MEM_TILES // UNC)
    def _(part):
        spread = jnp.int32(0)
        for k in range(UNC):
            t = part * UNC + k
            spread = jnp.maximum(spread, range_ref[P_HIGH, t] - range_ref[P_LOW, t])
            centre = centre_of(range_ref[P_LOW, t])
            left, right = lh_ref[t, 0:6, :], rh_ref[t, 0:6, :]
            lhs = own_features(left - centre[0:6], row8, 4.5)
            rhs, wb = right_features(right, centre, row8)
            wa = right_features(left, centre, row8)[1]
            out = jnp.dot(lhs, rhs, preferred_element_type=f32)
            store_forces(t, out[:TILE], out[TILE:], wa, wb)

        @pl.when(spread > 0)
        def _():
            @pl.loop(0, UNC)
            def _(k):
                t = part * UNC + k
                centre = centre_of(range_ref[P_LOW, t])
                left, right = lh_ref[t, 0:6, :], rh_ref[t, 0:6, :]
                wb, wa = right_features(right, centre, row8)[1], right_features(left, centre, row8)[1]
                live6 = row8 < 6
                a1, a2, a3 = split3(jnp.where(live6, lh_ref[t] - centre, 0.0) * scale)
                b1, b2, b3 = split3(jnp.where(live6, rh_ref[t] - centre, 0.0) * scale)
                one = jnp.ones_like(a1)
                left = jnp.concatenate([a1, a2, a3, one, one, one], axis=0).T.astype(bf16)
                diffs = []
                for c in range(6):
                    rhs = jnp.concatenate([unit[c], unit[c], unit[c], -b1 * unit[c], -b2 * unit[c], -b3 * unit[c]], axis=0).astype(bf16)
                    diffs.append(jnp.dot(left, rhs, preferred_element_type=f32))
                dx, dy, dz, du, dv, dw = diffs
                store_forces(t, dx * dx + dy * dy + dz * dz, dx * du + dy * dv + dz * dw, wa, wb)

    @pl.loop(0, MEM_TILES, unroll=UNC)
    def _(t):
        wb = sum_ref[1, t]
        con = lax.dot_general(wb, force_ref[0, t], NT, preferred_element_type=f32) + lax.dot_general(wb, force_ref[1, t], NT, preferred_element_type=f32)
        fo_ref[t, 0:8, :] = (lh_ref[t] - centre_of(range_ref[P_LOW, t])) * con[3:4] - (con[0:8] + con[8:16] + con[16:24])

    @pl.loop(0, MEM_TILES, unroll=UNC)
    def _(t):
        wa = sum_ref[0, t]
        rea = jnp.dot(wa, force_ref[0, t], preferred_element_type=f32) + jnp.dot(wa, force_ref[1, t], preferred_element_type=f32)
        fo_ref[t, 8:16, :] = (rh_ref[t] - centre_of(range_ref[P_LOW, t])) * rea[3:4] - (rea[0:8] + rea[8:16] + rea[16:24])

    def pieces_of(t):
        con, rea = fo_ref[t, 0:8, :], jnp.where(row8 < 3, fo_ref[t, 8:16, :], 0.0)
        c1 = con.astype(bf16).astype(f32)
        r1 = rea.astype(bf16).astype(f32)
        return (c1, con - c1), jnp.concatenate([r1, rea - r1], axis=0).astype(bf16)

    @pl.loop(0, MEM_TILES // UNS)
    def _(part):
        more = jnp.int32(0)
        sums = []
        for k in range(UNS):
            t = part * UNS + k
            con, rea = pieces_of(t)
            vert, index = ver_ref[pl.ds(t, 1), :], par_ref[pl.ds(t, 1), :]
            base = pl.multiple_of((range_ref[V_LOW, t] >> 3) << 3, 8)
            more = jnp.maximum(more, jnp.maximum(range_ref[P_HIGH, t] - range_ref[P_LOW, t], (range_ref[V_HIGH, t] - base) >> 4))
            sums.append((base, vertex_sums(base, vert & 127, vert >> 7, con, rowt, row16),
                         range_ref[P_LOW, t], partner_sums(range_ref[P_LOW, t], index & 127, index >> 7, rea, rowt)))
        for base, con, blk, rea in sums:
            add_vertex(con_ref, base, con)
            add_partner(rea_ref, blk, rea)

        @pl.when(more > 0)
        def _():
            @pl.loop(0, UNS)
            def _(k):
                t = part * UNS + k
                con, rea = pieces_of(t)
                vert, index = ver_ref[pl.ds(t, 1), :], par_ref[pl.ds(t, 1), :]
                base = (range_ref[V_LOW, t] >> 3) << 3

                @pl.loop(1, ((range_ref[V_HIGH, t] - base) >> 4) + 1)
                def _(j):
                    at = pl.multiple_of(base + j * SPAN, 8)
                    add_vertex(con_ref, at, vertex_sums(at, vert & 127, vert >> 7, con, rowt, row16))

                @pl.loop(range_ref[P_LOW, t] + 1, range_ref[P_HIGH, t] + 1)
                def _(blk):
                    add_partner(rea_ref, blk, partner_sums(blk, index & 127, index >> 7, rea, rowt))

    for load in loads[6:]:
        load.wait()
    width = out_ref.shape[1]
    for blk in range(-(-width // TILE)):
        at = slice(blk * TILE, min((blk + 1) * TILE, width))
        out_ref[:, at] = vel_ref[:, at] + TIME_STEP * (internal_ref[:, at] + con_ref[:, blk, :at.stop - at.start])
    held_copy.wait()

def contact(ranges, tab, mem, internal, vel, vertex, partner, index, count):
    arrays = ranges, mem, vertex, partner, index, tab, internal, vel
    hbm, vmem = pl.BlockSpec(memory_space=pltpu.HBM), pl.BlockSpec(memory_space=pltpu.VMEM)
    tile = pltpu.VMEM((MEM_TILES, 8, TILE), f32)
    held = jax.ShapeDtypeStruct((index.shape[0], 8, TILE), f32)
    return pl.pallas_call(
        contact_kernel,
        out_shape=(jax.ShapeDtypeStruct((9 * 3 * BOXES, TILE), f32), held, jax.ShapeDtypeStruct(vel.shape, f32)),
        in_specs=[pl.BlockSpec(memory_space=pltpu.SMEM)] + [hbm] * 8,
        out_specs=(vmem, hbm, vmem),
        scratch_shapes=[pltpu.VMEM((3, MB, TILE), f32), pltpu.VMEM(held.shape, f32), tile, tile, pltpu.VMEM((MEM_TILES, 16, TILE), f32),
                        pltpu.VMEM((2, MEM_TILES, TILE, TILE), bf16), pltpu.VMEM((2, MEM_TILES, 32, TILE), bf16),
                        pltpu.SemaphoreType.DMA((8,)), pltpu.SemaphoreType.DMA, pltpu.SMEM(ranges.shape, ranges.dtype)]
        + [pltpu.VMEM(x.shape, x.dtype) for x in arrays[1:]],
        compiler_params=pltpu.CompilerParams(vmem_limit_bytes=56 * 2**20),
        name="contact",
    )(count, *arrays)

BENDING_MODULUS = 20.0
AREA_MODULUS = 40.0

CHUNKS = 3

def block_range(index, unused):
    high = index >> 7
    full = index >= unused
    first = jnp.min(jnp.where(full, (unused >> 7) - 1, high).astype(f32).T, axis=0, keepdims=True)
    last = jnp.max(jnp.where(full, 0, high).astype(f32).T, axis=0, keepdims=True)
    return first.astype(jnp.int32), jnp.maximum(first, last).astype(jnp.int32)

def halo_kernel(nx, ny, *refs):
    arrays, (rest_ref, count_ref, tab_ref, mem_ref, internal_ref, range_ref) = refs[:8], refs[8:14]
    own_ref, x_ref, send_sem, recv_sem, own_sem, in_sem = refs[14:20]
    pos_ref, vel_ref, mpos_ref, mvel_ref, bend_ref, idx_ref, par_ref, ver_ref = local = refs[20:]
    gx, gy = lax.axis_index("gx"), lax.axis_index("gy")
    up, down = (lax.rem(gx + 1, nx), gy), (lax.rem(gx + nx - 1, nx), gy)
    right, left = (gx, lax.rem(gy + 1, ny)), (gx, lax.rem(gy + ny - 1, ny))
    size = own_ref.shape[0]
    part = size // CHUNKS

    barrier = pltpu.get_barrier_semaphore()
    for device in (up, down, right, left):
        pl.semaphore_signal(barrier, inc=1, device_id=device, device_id_type=MESH)
    loads = [pltpu.make_async_copy(array, ref, in_sem.at[k]) for k, (array, ref) in enumerate(zip(arrays, local))]
    for load in loads:
        load.start()
    loads[0].wait()
    loads[1].wait()
    for blk in range(BOXES):
        at = slice(blk * TILE, (blk + 1) * TILE)
        own_ref[pl.ds(blk, 3, stride=BOXES), :] = pos_ref[:, at]
        own_ref[pl.ds(3 * BOXES + blk, 3, stride=BOXES), :] = vel_ref[:, at]
    pl.semaphore_wait(barrier, 4)

    def slot(n, c):
        return tab_ref.at[pl.ds(n * size + c * part, part)]

    def copy(source, n, c, device):
        src = own_ref.at[pl.ds(c * part, part)] if source is None else slot(source, c)
        return pltpu.make_async_remote_copy(
            src_ref=src, dst_ref=slot(n, c), send_sem=send_sem.at[n, c], recv_sem=recv_sem.at[n, c],
            device_id=device, device_id_type=MESH)

    keep = pltpu.make_async_copy(own_ref, tab_ref.at[pl.ds(4 * size, size)], own_sem)
    keep.start()
    first = [[copy(None, 3, c, right), copy(None, 5, c, left)] for c in range(CHUNKS)]
    along = [[copy(None, 1, c, up), copy(None, 7, c, down)] for c in range(CHUNKS)]
    on = [[copy(3, 0, c, up), copy(3, 6, c, down), copy(5, 2, c, up), copy(5, 8, c, down)] for c in range(CHUNKS)]
    for c in range(CHUNKS):
        for one in first[c] + along[c]:
            one.start()

    def forward(c):
        for k in range(2):
            first[c][k].wait_recv()
            on[c][2 * k].start()
            on[c][2 * k + 1].start()

    for k in (2, 3, 5, 6, 7):
        loads[k].wait()
    width = mpos_ref.shape[1]
    rows = mem_ref.shape[0] // 6
    mem_ref[...] = jnp.zeros_like(mem_ref)
    for blk in range(-(-width // TILE)):
        at = slice(blk * TILE, min((blk + 1) * TILE, width))
        mem_ref[pl.ds(blk, 3, stride=rows), :at.stop - at.start] = mpos_ref[:, at]
        mem_ref[pl.ds(3 * rows + blk, 3, stride=rows), :at.stop - at.start] = mvel_ref[:, at]
    range_ref[...] = jnp.zeros_like(range_ref)
    parts = idx_ref.shape[0] // TILE
    for k in range(parts):
        range_ref[k:k + 1, :], range_ref[parts + k:parts + k + 1, :] = block_range(idx_ref[k * TILE:(k + 1) * TILE, :], 9 * BOXES * TILE)
    for k, ref in ((P_LOW, par_ref), (V_LOW, ver_ref)):
        low, high = block_range(ref[...], 9 * BOXES * TILE)
        range_ref[k:k + 1, :low.shape[1]] = low
        range_ref[k + 1:k + 2, :low.shape[1]] = high
    forward(0)
    cells = x_ref.shape[0] // 3
    for d in range(3):
        for j in range(cells):
            x_ref[d * cells + j:d * cells + j + 1, :] = mpos_ref[d:d + 1, j * V:(j + 1) * V]
    x = x_ref[...]
    relative = x - jnp.sum(x, axis=1, keepdims=True) * (1.0 / V)
    loads[4].wait()
    once = lax.dot_general(relative, bend_ref[...], NT, precision=lax.Precision.HIGHEST, preferred_element_type=f32)
    forward(1)
    twice = lax.dot_general(once, bend_ref[...], NT, precision=lax.Precision.HIGHEST, preferred_element_type=f32)
    forward(2)
    square = jnp.sum(relative * relative, axis=1, keepdims=True)
    spread = (square[:cells] + square[cells:2 * cells] + square[2 * cells:]) * (1.0 / V)
    slot_row = lax.broadcasted_iota(jnp.int32, (cells, 1), 0)
    rest = jnp.ones((cells, 1), f32)
    for j in range(cells):
        rest = jnp.where(slot_row == j, rest_ref[j], rest)
    stretch = AREA_MODULUS * (spread / rest - 1.0)
    alive = (slot_row < count_ref[0]).astype(f32)
    for d in range(3):
        rows = slice(d * cells, (d + 1) * cells)
        x_ref[rows] = -(BENDING_MODULUS * twice[rows] + stretch * relative[rows]) * alive
    for d in range(3):
        for j in range(cells):
            internal_ref[d:d + 1, j * V:(j + 1) * V] = x_ref[d * cells + j:d * cells + j + 1, :]

    keep.wait()
    for c in range(CHUNKS):
        for one in first[c]:
            one.wait_send()
        for one in along[c] + on[c]:
            one.wait()

def halo(pos, vel, mpos, mvel, bending, index, partner, vertex, rest, count):
    size = 6 * BOXES
    arrays = pos, vel, mpos, mvel, bending, index, partner, vertex
    nx, ny = lax.axis_size("gx"), lax.axis_size("gy")
    vmem, anywhere = pl.BlockSpec(memory_space=pltpu.VMEM), pl.BlockSpec(memory_space=pl.ANY)
    return pl.pallas_call(
        functools.partial(halo_kernel, nx, ny),
        out_shape=(
            jax.ShapeDtypeStruct((9 * size, TILE), f32),
            jax.ShapeDtypeStruct((6 * MB, TILE), f32),
            jax.ShapeDtypeStruct(mpos.shape, f32),
            jax.ShapeDtypeStruct((16, TILE), jnp.int32),
        ),
        in_specs=[pl.BlockSpec(memory_space=pltpu.HBM)] * 8 + [pl.BlockSpec(memory_space=pltpu.SMEM)] * 2,
        out_specs=(anywhere, vmem, vmem, vmem),
        scratch_shapes=[pltpu.VMEM((size, TILE), f32), pltpu.VMEM((3 * rest.shape[0], V), f32),
                        pltpu.SemaphoreType.DMA((9, CHUNKS)), pltpu.SemaphoreType.DMA((9, CHUNKS)), pltpu.SemaphoreType.DMA,
                        pltpu.SemaphoreType.DMA((8,))] + [pltpu.VMEM(x.shape, x.dtype) for x in arrays],
        compiler_params=pltpu.CompilerParams(collective_id=0, has_side_effects=True, vmem_limit_bytes=56 * 2**20),
        name="halo",
    )(*arrays, rest, count)

def on_device(solvent_pos, solvent_vel, pair_index, random_pairs, membrane_pos, membrane_vel, mem_vertex, mem_partner,
              bending, rest_size, cell_count):
    tab, mem, internal, ranges = halo(solvent_pos, solvent_vel, membrane_pos, membrane_vel, bending, pair_index, mem_partner,
                                      mem_vertex, rest_size, cell_count)
    rea, held, membrane_velocity = contact(ranges, tab, mem, internal, membrane_vel, mem_vertex, mem_partner, pair_index, cell_count)
    solvent_velocity = pairs(held, random_pairs, tab, rea).reshape(3, BOXES * TILE)
    return solvent_velocity, membrane_velocity

def solution(mesh):
    both = ("gx", "gy")
    flat, tiles = P(None, both), P(both, None)
    return jax.shard_map(
        on_device,
        mesh=mesh,
        in_specs=(flat, flat, tiles, P(both, None, None), flat, flat, tiles, tiles, P(), P(both), P(both)),
        out_specs=(flat, flat),
        check_vma=False,
    )
```
